512 devices in a mesh: fsdp: 64 (over x, z_lo, core), col: 8 (over z_hi, y).
Axes of the slice: x: 4, y: 4, z: 16 (z_hi: 2, z_lo: 8; z = z_hi * 8 + z_lo), core: 2. Of those that a mesh axis runs over, the one named last changes fastest.
Arguments:
- codes: bfloat16 [8192, 26624], P('fsdp', 'col'), may hold values from -96 to 96
- scales: float32 [64, 208], P('fsdp', 'col'), may hold values from 0.01 to 0.1
- factors: float32 [7, 8192, 64], P(None, 'fsdp'), may hold values from -0.225 to 0.225
- upstream: bfloat16 [8192, 26624], P('fsdp', 'col'), may hold values from -0.036621094 to 0.036621094
Outputs:
- factor_grads: float32 [7, 8192, 64], P(None, 'fsdp')
The draws below stay inside these ranges and needn't reach their ends.
All inputs are finite; a program needn't handle non-finite values.
Results may differ from the reference program's by a relative error of at most 0.02.
Values may be sent and summed in bfloat16 or wider, within the bound.
No kernel may reach another device: no remote copies, remote signals or barrier semaphores. Data moves between devices by JAX's collectives and lax.ppermute only.
A program may use at most 64 MiB of HBM per device.

```python
import math
import jax
import jax.numpy as jnp
from jax import lax

D = 8192
COLS = 26624
BLOCK = 64
LEVELS = 7
SCALE_BLK = 128


def block_levels(key, extent, shards, low, largest):
    loudness, own = 1.0, jax.random.fold_in(key, 6)
    for dim, blocks in shards:
        draws = jnp.exp(jax.random.uniform(jax.random.fold_in(own, dim), (blocks,), jnp.float32, low / len(shards), largest / len(shards)))
        loudness = loudness * jnp.repeat(draws, extent[dim] // blocks).reshape([-1 if axis == dim else 1 for axis in range(len(extent))])
    return loudness


def scatter_about(stream_key, shape, scale, most, pieces=(), kind=jnp.bfloat16):
    drawn = scale * jax.random.normal(stream_key, shape, jnp.float32)
    if pieces:
        drawn = drawn * block_levels(stream_key, shape, pieces, -0.22, 0.18)
    return jnp.clip(drawn, -most, most).astype(kind)


def setup_inputs(seed: int = 0) -> dict:
    arg_keys = jax.random.split(jax.random.key(seed), 5)
    return {
        "codes": scatter_about(arg_keys[0], (D, COLS), 16.0, 96.0, ((0, 64), (1, 8))),
        "scales": jnp.clip(jnp.exp(math.log(0.1) - 2.3025851 * jax.random.uniform(arg_keys[1], (D // SCALE_BLK, COLS // SCALE_BLK), jnp.float32) ** block_levels(arg_keys[1], (D // SCALE_BLK, COLS // SCALE_BLK), ((0, 64), (1, 8)), -0.2, 0.2)), 0.01, 0.1),
        "factors": scatter_about(arg_keys[2], (LEVELS, D, BLOCK), (0.3 * BLOCK ** -0.5), 0.225, ((1, 64),), jnp.float32),
        "upstream": scatter_about(arg_keys[3], (D, COLS), (COLS ** -0.5), 0.036621094, ((0, 64), (1, 8))),
    }


def rows_eye(first, count, distance):
    half = BLOCK // 2
    rows = first + jnp.arange(count, dtype=jnp.int32)
    pick = ((rows // distance) % 2) * half + rows % half
    return (jnp.arange(BLOCK, dtype=jnp.int32)[None, :] == pick[:, None]).astype(jnp.float32)


def forward_level(mixing, values, distance, count):
    half = BLOCK // 2
    groups = count // (2 * distance)
    parts = distance // half
    wide = values.shape[1]
    mats = mixing.astype(jnp.float32).reshape(groups, 2, parts, half, 2, half)
    vecs = values.astype(jnp.float32).reshape(groups, 2, parts, half, wide)
    out = jnp.einsum("ghqtHs,gHqsc->ghqtc", mats, vecs)
    return out.reshape(count, wide).astype(jnp.bfloat16)


def backward_level(mixing, values, grad, distance, count):
    half = BLOCK // 2
    groups = count // (2 * distance)
    parts = distance // half
    wide = values.shape[1]
    mats = mixing.astype(jnp.float32).reshape(groups, 2, parts, half, 2, half)
    vecs = values.astype(jnp.float32).reshape(groups, 2, parts, half, wide)
    grads = grad.astype(jnp.float32).reshape(groups, 2, parts, half, wide)
    dmix = jnp.einsum("ghqtc,gHqsc->ghqtHs", grads, vecs).reshape(count, BLOCK)
    lower = jnp.einsum("gqtHs,gqtc->gHqsc", mats[:, 0], grads[:, 0]).astype(jnp.bfloat16)
    upper = jnp.einsum("gqtHs,gqtc->gHqsc", mats[:, 1], grads[:, 1]).astype(jnp.bfloat16)
    lower, upper = lax.optimization_barrier((lower, upper))
    back = (lower.astype(jnp.float32) + upper.astype(jnp.float32)).reshape(count, wide).astype(jnp.bfloat16)
    return dmix, back


def reference(codes, scales, factors, upstream):
    half = BLOCK // 2
    mixing = [(rows_eye(0, D, half * 2 ** level) + factors[level]).astype(jnp.bfloat16) for level in range(LEVELS)]
    width = math.gcd(COLS, 1024)
    count = COLS // width

    def one_slab(index, total):
        start = (index * width).astype(jnp.int32)
        piece = lax.dynamic_slice_in_dim(codes, start, width, 1).astype(jnp.float32)
        sstart = (index * (width // SCALE_BLK)).astype(jnp.int32)
        spiece = lax.dynamic_slice_in_dim(scales, sstart, width // SCALE_BLK, 1)
        base = piece.reshape(D // SCALE_BLK, SCALE_BLK, width // SCALE_BLK, SCALE_BLK) * spiece[:, None, :, None]
        values = base.reshape(D, width).astype(jnp.bfloat16)
        saved = []
        for level in range(LEVELS):
            saved.append(values)
            values = forward_level(mixing[level], values, half * 2 ** level, D)
        grad = lax.dynamic_slice_in_dim(upstream, start, width, 1)
        grads = []
        for level in reversed(range(LEVELS)):
            dmix, grad = backward_level(mixing[level], saved[level], grad, half * 2 ** level, D)
            grads.append(dmix)
        grads = grads[::-1]
        return total + jnp.stack(grads)

    start_total = jnp.zeros((LEVELS, D, BLOCK), jnp.float32)
    return lax.fori_loop(0, count, one_slab, start_total)
```

```python
import functools

import jax
import jax.numpy as jnp
from jax import lax
from jax.experimental import pallas as pl
from jax.experimental.pallas import tpu as pltpu
from jax.sharding import Mesh
from jax.sharding import PartitionSpec as P

BF = jnp.bfloat16
F32 = jnp.float32
HALF = 32
ROWS = 128
LEVELS = 7


def dot(a, b):
    return lax.dot_general(a, b, (((1,), (0,)), ((), ())), preferred_element_type=F32)


def dot_nt(a, b):
    return lax.dot_general(a, b, (((1,), (1,)), ((), ())), preferred_element_type=F32)


def pair(p, bit):
    low = (p >> bit << (bit + 1)) | (p & ((1 << bit) - 1))
    return low, low | (1 << bit)


def iota(shape, dim):
    return lax.broadcasted_iota(jnp.int32, shape, dim)


def spread(m, level):
    width = ROWS if level < 2 else 2 * ROWS
    src, col = iota((2 * HALF, width), 0), iota((2 * HALF, width), 1)
    r, c = iota((ROWS, width), 0), iota((ROWS, width), 1)
    if level == 0:
        pick = src == col % 64
        keep = r // 64 == c // 64
    elif level == 1:
        pick = src == col // 64 * HALF + col % HALF
        keep = (r // HALF) % 2 == (c // HALF) % 2
    else:
        pick = src == col // ROWS * HALF + col % HALF
        keep = r // HALF == (c // HALF) % 4
    dense = dot(m, pick.astype(F32).astype(BF))
    return jnp.where(keep, dense, 0.0).astype(BF)


def grad_kernel(blocks, mix, far_mix, mine, theirs, grads, dense, state):
    step = pl.program_id(0)

    def top():
        r, c = iota((ROWS, ROWS), 0), iota((ROWS, ROWS), 1)
        keep = r // HALF == c // HALF
        pick = (iota((HALF, ROWS), 0) == iota((HALF, ROWS), 1) % HALF).astype(F32).astype(BF)

        def body(b, carry):
            near = jnp.where(keep, dot(far_mix[0, b], pick), 0.0).astype(BF)
            far = jnp.where(keep, dot(far_mix[1, b], pick), 0.0).astype(BF)
            both = jnp.concatenate([mine[b], theirs[b]], axis=1)
            out = dot(both, jnp.concatenate([near, far], axis=0)).astype(BF)
            state[b] = out
            grads[0, b] = out
            return carry

        lax.fori_loop(0, blocks, body, 0)

    def wide(level):
        def body(p, carry):
            lo, hi = pair(p, level - 2)
            dlo, dhi = spread(mix[0, lo], level), spread(mix[0, hi], level)
            dense[0, lo], dense[0, hi] = dlo, dhi
            both = jnp.concatenate([state[lo], state[hi]], axis=1)
            out = dot(both, jnp.concatenate([dlo, dhi], axis=0)).astype(BF)
            state[lo], state[hi] = out[:, :ROWS], out[:, ROWS:]
            grads[0, lo], grads[0, hi] = out[:, :ROWS], out[:, ROWS:]
            return carry

        lax.fori_loop(0, blocks // 2, body, 0)

    def narrow(level):
        def body(b, carry):
            d = spread(mix[0, b], level)
            dense[0, b, :, :ROWS] = d
            if level:
                out = dot(state[b], d).astype(BF)
                grads[0, b] = out
            return carry

        lax.fori_loop(0, blocks, body, 0)

    for s in range(LEVELS):
        level = LEVELS - 1 - s
        pl.when(step == s)(top if s == 0 else functools.partial(wide if level > 1 else narrow, level))


def grad_chain(mix, top_mix, mine, theirs):
    blocks, wide, rows = mine.shape
    last = LEVELS - 1
    return pl.pallas_call(
        functools.partial(grad_kernel, blocks),
        grid=(LEVELS,),
        in_specs=[
            pl.BlockSpec((1, blocks, rows, 2 * HALF), lambda s: (jnp.minimum(last - s, last - 1), 0, 0, 0)),
            pl.BlockSpec(memory_space=pltpu.VMEM),
            pl.BlockSpec(memory_space=pltpu.VMEM),
            pl.BlockSpec(memory_space=pltpu.VMEM),
        ],
        out_specs=[
            pl.BlockSpec((1, blocks, wide, rows), lambda s: (jnp.maximum(last - 1 - s, 0), 0, 0, 0)),
            pl.BlockSpec((1, blocks, rows, 2 * rows), lambda s: (jnp.minimum(last - s, last - 1), 0, 0, 0)),
        ],
        out_shape=[
            jax.ShapeDtypeStruct((last, blocks, wide, rows), BF),
            jax.ShapeDtypeStruct((last, blocks, rows, 2 * rows), BF),
        ],
        scratch_shapes=[pltpu.VMEM((blocks, wide, rows), BF)],
        compiler_params=pltpu.CompilerParams(vmem_limit_bytes=40 * 2**20),
        name="grad_chain",
    )(mix, top_mix, mine, theirs)


def fold(quad):
    lane = iota((HALF, ROWS), 1) // HALF
    out = quad[:HALF]
    for q in range(1, 4):
        out = jnp.where(lane == q, quad[q * HALF : (q + 1) * HALF], out)
    return out


def score_kernel(blocks, base, dense, grads, mine, theirs, out, state):
    level = pl.program_id(0)
    rows = ROWS

    def first():
        eye = (iota((rows, rows), 0) == iota((rows, rows), 1)).astype(F32).astype(BF)

        def body(b, carry):
            x = dot_nt(eye, base[b]).astype(BF)
            quad = dot(x, grads[0, b])
            lane = iota((64, rows), 1) // 64
            out[b, 0] = jnp.where(lane == 0, quad[:64], quad[64:]).astype(BF)
            state[b] = dot(dense[0, b, :, :rows], x).astype(BF)
            return carry

        lax.fori_loop(0, blocks, body, 0)

    def second():
        def body(b, carry):
            x = state[b]
            quad = dot(x, grads[0, b])
            lane = (iota((HALF, rows), 1) // HALF) % 2
            out[b, 0, :HALF] = jnp.where(lane == 0, quad[:HALF], quad[HALF : 2 * HALF]).astype(BF)
            out[b, 0, HALF:] = jnp.where(lane == 0, quad[2 * HALF : 3 * HALF], quad[3 * HALF :]).astype(BF)
            state[b] = dot(dense[0, b, :, :rows], x).astype(BF)
            return carry

        lax.fori_loop(0, blocks, body, 0)

    def wide(lev):
        def body(p, carry):
            lo, hi = pair(p, lev - 2)
            x = jnp.concatenate([state[lo], state[hi]], axis=0)
            g = jnp.concatenate([grads[0, lo], grads[0, hi]], axis=1)
            quad = dot(x, g)
            for k, b in enumerate((lo, hi)):
                for h in range(2):
                    part = fold(quad[h * rows : (h + 1) * rows, k * rows : (k + 1) * rows])
                    out[b, 0, h * HALF : (h + 1) * HALF] = part.astype(BF)
            y = dot(jnp.concatenate([dense[0, lo], dense[0, hi]], axis=0), x).astype(BF)
            state[lo], state[hi] = y[:rows], y[rows:]
            return carry

        lax.fori_loop(0, blocks // 2, body, 0)

    def top():
        def body(b, carry):
            quad = dot(state[b], jnp.concatenate([mine[b], theirs[b]], axis=1))
            out[b, 0, :HALF] = fold(quad[:, :rows]).astype(BF)
            out[b, 0, HALF:] = fold(quad[:, rows:]).astype(BF)
            return carry

        lax.fori_loop(0, blocks, body, 0)

    for lev in range(LEVELS):
        body = first if lev == 0 else second if lev == 1 else top if lev == LEVELS - 1 else functools.partial(wide, lev)
        pl.when(level == lev)(body)


def scores(base, dense, grads, mine, theirs):
    blocks, wide, rows = base.shape
    last = LEVELS - 1
    return pl.pallas_call(
        functools.partial(score_kernel, blocks),
        grid=(LEVELS,),
        in_specs=[
            pl.BlockSpec(memory_space=pltpu.VMEM),
            pl.BlockSpec((1, blocks, rows, 2 * rows), lambda s: (jnp.minimum(s, last - 1), 0, 0, 0)),
            pl.BlockSpec((1, blocks, wide, rows), lambda s: (jnp.minimum(s, last - 1), 0, 0, 0)),
            pl.BlockSpec(memory_space=pltpu.VMEM),
            pl.BlockSpec(memory_space=pltpu.VMEM),
        ],
        out_specs=pl.BlockSpec((blocks, 1, 2 * HALF, rows), lambda s: (0, s, 0, 0)),
        out_shape=jax.ShapeDtypeStruct((blocks, LEVELS, 2 * HALF, rows), BF),
        scratch_shapes=[pltpu.VMEM((blocks, rows, wide), BF)],
        compiler_params=pltpu.CompilerParams(vmem_limit_bytes=40 * 2**20),
        name="scores",
    )(base, dense, grads, mine, theirs)


def flips(count, distance=1):
    return [(i, i ^ distance) for i in range(count)]


def per_device(codes, scales, factors, upstream):
    rows, wide = codes.shape
    nz, ny = lax.axis_size("z"), lax.axis_size("y")
    blocks = 2 * nz
    chunk = wide // blocks
    side = lax.axis_index("x0")
    core = lax.axis_index("core")
    me_y = lax.axis_index("y")
    first = ((lax.axis_index("x1") * 2 + side) * nz + lax.axis_index("z")) * 2 * rows + core * rows

    mine = lax.all_to_all(upstream.T.reshape(blocks, chunk, rows), ("z", "core"), 0, 0)
    base = (
        codes.astype(F32).reshape(rows, wide // rows, rows) * scales[0][None, :, None]
    ).reshape(rows, wide).astype(BF)
    base = lax.all_to_all(base.T.reshape(blocks, chunk, rows), ("z", "core"), 0, 0)
    theirs = lax.ppermute(mine, "x0", flips(2))

    row = first + jnp.arange(rows, dtype=jnp.int32)
    mixing = []
    for level in range(LEVELS):
        pick = row // (HALF * 2**level) % 2 * HALF + row % HALF
        eye = (jnp.arange(2 * HALF, dtype=jnp.int32)[None, :] == pick[:, None]).astype(F32)
        mixing.append((eye + factors[level]).astype(BF))
    mix = lax.all_gather(jnp.stack(mixing), ("z", "core"), axis=1)
    last = mix[LEVELS - 1]
    send = jnp.where(side == 0, last[..., HALF:], last[..., :HALF])
    keep = jnp.where(side == 0, last[..., :HALF], last[..., HALF:])
    top_mix = jnp.stack([keep, lax.ppermute(send, "x0", flips(2))])

    grads, dense = grad_chain(mix[: LEVELS - 1], top_mix, mine, theirs)
    parts = scores(base, dense, grads, mine, theirs)

    far = lax.ppermute(parts[:, LEVELS - 1, HALF:], "x0", flips(2))
    near = parts[:, LEVELS - 1, :HALF]
    top = jnp.concatenate([jnp.where(side == 0, near, far), jnp.where(side == 0, far, near)], axis=1)
    parts = jnp.concatenate([parts[:, : LEVELS - 1], top[:, None]], axis=1)

    parts = parts.reshape(nz, 2, LEVELS, 2 * HALF, rows)
    own = lax.dynamic_index_in_dim(parts, core, 1, keepdims=False)
    away = lax.dynamic_index_in_dim(parts, 1 - core, 1, keepdims=False)
    total = own.astype(F32) + lax.ppermute(away, "core", flips(2)).astype(F32)
    total = total.astype(BF).reshape(nz, LEVELS, ny, 2 * HALF // ny, rows).transpose(2, 0, 1, 3, 4)
    total = jnp.sum(lax.all_to_all(total, "y", 0, 0).astype(F32), axis=0).astype(BF)
    total = jnp.sum(lax.all_to_all(total, "z", 0, 0).astype(F32), axis=0)
    total = total + lax.ppermute(total, "zh", flips(2))
    total = lax.all_gather(total, "y", axis=1)
    return total.reshape(LEVELS, 2 * HALF, rows).transpose(0, 2, 1)


def solution(mesh):
    fsdp, col = mesh.devices.shape
    nz = 8
    names = ("x1", "x0", "z", "core", "zh", "y")
    fine = Mesh(mesh.devices.reshape(fsdp // (4 * nz), 2, nz, 2, 2, col // 2), names)
    rows, cols = ("x1", "x0", "z", "core"), ("zh", "y")
    return jax.shard_map(
        per_device,
        mesh=fine,
        in_specs=(P(rows, cols), P(rows, cols), P(None, rows, None), P(rows, cols)),
        out_specs=P(None, rows, None),
        check_vma=False,
    )
```

```python
import functools

import jax
import jax.numpy as jnp
from jax import lax
from jax.experimental import pallas as pl
from jax.experimental.pallas import tpu as pltpu
from jax.sharding import Mesh
from jax.sharding import PartitionSpec as P

BF = jnp.bfloat16
F32 = jnp.float32
HALF = 32
BLOCK = 2 * HALF
ROWS = 128
LEVELS = 7
TOP = LEVELS - 1
NZ = 8
NY = 4
SLICE = BLOCK // NY
PARAMS = pltpu.CompilerParams(vmem_limit_bytes=58 * 2**20)
WHOLE = pl.BlockSpec(memory_space=pltpu.VMEM)
SCALARS = pl.BlockSpec(memory_space=pltpu.SMEM)


def dot(a, b):
    return lax.dot_general(a, b, (((1,), (0,)), ((), ())), preferred_element_type=F32)


def dot_nt(a, b):
    return lax.dot_general(a, b, (((1,), (1,)), ((), ())), preferred_element_type=F32)


def iota(shape, dim):
    return lax.broadcasted_iota(jnp.int32, shape, dim)


def flips(count, distance=1):
    return [(i, i ^ distance) for i in range(count)]


def units(level):
    if level == 2:
        return [[(2 * z, 2 * z + 1)] for z in range(NZ)]
    if level < 2 or level == TOP:
        return [[(2 * z, None), (2 * z + 1, None)] for z in range(NZ)]
    bit = level - 3
    lows = [z for z in range(NZ) if not z >> bit & 1]
    return [[(2 * z + c, 2 * (z | 1 << bit) + c) for c in range(2)] for z in lows]


def pack_kernel(me, upstream, factors, out):
    chunk = out.shape[1] - BLOCK
    for t in range(upstream.shape[1] // ROWS):
        turned = upstream[:, t * ROWS : (t + 1) * ROWS].T
        start, end = t * ROWS, (t + 1) * ROWS
        while start < end:
            block, at = start // chunk, start % chunk
            size = min(end - start, chunk - at)
            out[block, at : at + size] = turned[start - t * ROWS : start - t * ROWS + size]
            start += size
    row = me[4] + iota((ROWS, BLOCK), 0)
    tile = jnp.zeros((ROWS, ROWS), F32)
    for side in range(2):
        level = jnp.minimum(2 * me[0] + side, TOP)
        pick = lax.shift_right_logical(row, level + 5) % 2 * HALF + row % HALF
        eye = (iota((ROWS, BLOCK), 1) == pick).astype(F32)
        place = (iota((BLOCK, ROWS), 1) == iota((BLOCK, ROWS), 0) + side * BLOCK).astype(F32).astype(BF)
        tile = tile + dot((eye + factors[level]).astype(BF), place)
    tile = tile.astype(BF)
    for block in range(out.shape[0]):
        half = block % 2 * BLOCK
        out[block, chunk:] = tile[half : half + BLOCK]


def pack(me, upstream, factors):
    rows, wide = upstream.shape
    return pl.pallas_call(
        pack_kernel,
        in_specs=[SCALARS, WHOLE, WHOLE],
        out_specs=WHOLE,
        out_shape=jax.ShapeDtypeStruct((2 * NZ, wide // (2 * NZ) + BLOCK, rows), BF),
        compiler_params=PARAMS,
        name="pack",
    )(me, upstream, factors)


def expand_kernel(me, near, away, dense):
    my_y, my_core, my_x = me[0], me[2], me[3]

    def run(level):
        width = ROWS if level < 2 else 2 * ROWS
        src, col = iota((ROWS, width), 0), iota((ROWS, width), 1)
        lane = level % 2 * BLOCK
        if level == 0:
            pick = src == lane + col % BLOCK
        elif level == 1:
            pick = src == lane + col // BLOCK * HALF + col % HALF
        elif level < TOP:
            pick = src == lane + col // ROWS * HALF + col % HALF
        else:
            pick = src == HALF * my_x + col // ROWS * BLOCK + col % HALF
        pick = pick.astype(F32).astype(BF)
        which = jnp.bitwise_xor(my_y, level // 2)
        for c, ref in enumerate((near, away)):
            at = pl.multiple_of(jnp.bitwise_xor(my_core, c) * BLOCK, BLOCK)
            row, col = at + iota((BLOCK, width), 0), iota((BLOCK, width), 1)
            if level == 0:
                keep = row // BLOCK == col // BLOCK
            elif level == 1:
                keep = (row // HALF) % 2 == (col // HALF) % 2
            else:
                keep = row // HALF == (col // HALF) % 4
            for block in range(2 * NZ):
                full = jnp.where(keep, dot(ref[which, block], pick), 0.0).astype(BF)
                dense[0, block, pl.ds(at, BLOCK), :width] = full

    for level in range(LEVELS):
        pl.when(pl.program_id(0) == level)(functools.partial(run, level))


def expand(me, near, away):
    shape = (2 * NZ, ROWS, 2 * ROWS)
    return pl.pallas_call(
        expand_kernel,
        grid=(LEVELS,),
        in_specs=[SCALARS, WHOLE, WHOLE],
        out_specs=pl.BlockSpec((1,) + shape, lambda s: (s, 0, 0, 0)),
        out_shape=jax.ShapeDtypeStruct((LEVELS,) + shape, BF),
        compiler_params=PARAMS,
        name="expand",
    )(me, near, away)


def grad_kernel(dense, mine, theirs, grads, state):
    def run(level):
        for unit in units(level):
            for lo, hi in unit:
                if level == TOP:
                    both = jnp.concatenate([mine[lo], theirs[lo]], axis=1)
                    full = jnp.concatenate([dense[0, lo, :, :ROWS], dense[0, lo, :, ROWS:]], axis=0)
                elif level == 1:
                    both, full = state[lo], dense[0, lo, :, :ROWS]
                else:
                    both = jnp.concatenate([state[lo], state[hi]], axis=1)
                    full = jnp.concatenate([dense[0, lo], dense[0, hi]], axis=0)
                out = dot(both, full).astype(BF)
                grads[0, lo] = out[:, :ROWS]
                if level > 1:
                    state[lo] = out[:, :ROWS]
                if hi is not None:
                    grads[0, hi] = out[:, ROWS:]
                    state[hi] = out[:, ROWS:]

    for s in range(TOP):
        pl.when(pl.program_id(0) == s)(functools.partial(run, TOP - s))


def grad_chain(dense, mine, theirs):
    blocks, wide, rows = mine.shape
    return pl.pallas_call(
        grad_kernel,
        grid=(TOP,),
        in_specs=[pl.BlockSpec((1, blocks, rows, 2 * rows), lambda s: (TOP - s, 0, 0, 0)), WHOLE, WHOLE],
        out_specs=pl.BlockSpec((1, blocks, wide, rows), lambda s: (TOP - 1 - s, 0, 0, 0)),
        out_shape=jax.ShapeDtypeStruct((TOP, blocks, wide, rows), BF),
        scratch_shapes=[pltpu.VMEM((blocks, wide, rows), BF)],
        compiler_params=PARAMS,
        name="grad_chain",
    )(dense, mine, theirs)


def fold(quad):
    lane = iota((HALF, ROWS), 1) // HALF
    out = quad[:HALF]
    for q in range(1, 4):
        out = jnp.where(lane == q, quad[q * HALF : (q + 1) * HALF], out)
    return out


def score_kernel(me, base, dense, grads, mine, theirs, own, away, state):
    first_core = me[2] == 0

    def store(z, parts):
        zero, one = parts
        mine_, other = jnp.where(first_core, zero, one), jnp.where(first_core, one, zero)
        for y in range(NY):
            own[y, z, 0] = mine_[y * SLICE : (y + 1) * SLICE].astype(BF)
            away[y, z, 0] = other[y * SLICE : (y + 1) * SLICE].astype(BF)

    def run(level):
        if level == 0:
            eye = (iota((ROWS, ROWS), 0) == iota((ROWS, ROWS), 1)).astype(F32).astype(BF)
        for unit in units(level):
            parts = {}
            for lo, hi in unit:
                if level == 0:
                    x = dot_nt(eye, base[lo]).astype(BF)
                elif hi is None:
                    x = state[lo]
                else:
                    x = jnp.concatenate([state[lo], state[hi]], axis=0)
                if level == TOP:
                    g = jnp.concatenate([mine[lo], theirs[lo]], axis=1)
                elif hi is None:
                    g = grads[0, lo]
                else:
                    g = jnp.concatenate([grads[0, lo], grads[0, hi]], axis=1)
                quad = dot(x, g)
                if level == 0:
                    parts[lo] = jnp.where(iota((BLOCK, ROWS), 1) < BLOCK, quad[:BLOCK], quad[BLOCK:])
                elif level == 1:
                    even = (iota((HALF, ROWS), 1) // HALF) % 2 == 0
                    rows = [quad[q * HALF : (q + 1) * HALF] for q in range(4)]
                    parts[lo] = jnp.concatenate([jnp.where(even, rows[0], rows[1]), jnp.where(even, rows[2], rows[3])], axis=0)
                elif level == TOP:
                    parts[lo] = jnp.concatenate([fold(quad[:, :ROWS]), fold(quad[:, ROWS:])], axis=0)
                else:
                    for b, at in ((lo, slice(0, ROWS)), (hi, slice(ROWS, 2 * ROWS))):
                        parts[b] = jnp.concatenate([fold(quad[:ROWS, at]), fold(quad[ROWS:, at])], axis=0)
                if level < 2:
                    state[lo] = dot(dense[0, lo, :, :ROWS], x).astype(BF)
                elif level < TOP:
                    full = jnp.concatenate([dense[0, lo], dense[0, hi]], axis=0)
                    out = dot(full, x).astype(BF)
                    state[lo], state[hi] = out[:ROWS], out[ROWS:]
            for z in sorted({b // 2 for b in parts}):
                store(z, (parts[2 * z], parts[2 * z + 1]))

    for level in range(LEVELS):
        pl.when(pl.program_id(0) == level)(functools.partial(run, level))


def scores(me, base, dense, grads, mine, theirs):
    blocks, wide, rows = base.shape
    shape = (NY, NZ, LEVELS, SLICE, rows)
    out_spec = pl.BlockSpec((NY, NZ, 1, SLICE, rows), lambda s: (0, 0, s, 0, 0))
    return pl.pallas_call(
        score_kernel,
        grid=(LEVELS,),
        in_specs=[
            SCALARS,
            WHOLE,
            pl.BlockSpec((1, blocks, rows, 2 * rows), lambda s: (jnp.minimum(s, TOP - 1), 0, 0, 0)),
            pl.BlockSpec((1, blocks, wide, rows), lambda s: (jnp.minimum(s, TOP - 1), 0, 0, 0)),
            WHOLE,
            WHOLE,
        ],
        out_specs=[out_spec, out_spec],
        out_shape=[jax.ShapeDtypeStruct(shape, BF)] * 2,
        scratch_shapes=[pltpu.VMEM((blocks, rows, wide), BF)],
        compiler_params=PARAMS,
        name="scores",
    )(me, base, dense, grads, mine, theirs)


def core_sum_kernel(me, own, got, *outs):
    for k, out in enumerate(outs):
        y = jnp.bitwise_xor(me[0], k)
        out[...] = (own[y].astype(F32) + got[y].astype(F32)).astype(BF)


def core_sum(me, own, got):
    return pl.pallas_call(
        core_sum_kernel,
        in_specs=[SCALARS, WHOLE, WHOLE],
        out_specs=[WHOLE] * NY,
        out_shape=[jax.ShapeDtypeStruct(own.shape[1:], BF)] * NY,
        compiler_params=PARAMS,
        name="core_sum",
    )(me, own, got)


def finish_kernel(me, *refs):
    *pieces, out, rows = refs
    for k, piece in enumerate(pieces):
        y = jnp.bitwise_xor(me[0], k)
        rows[:, pl.ds(pl.multiple_of(y * SLICE, SLICE), SLICE), :] = piece[...]
    for level in range(TOP):
        out[level] = rows[level].T
    last = rows[TOP]
    swapped = jnp.concatenate([last[HALF:], last[:HALF]], axis=0)
    out[TOP] = jnp.where(me[3] == 0, last, swapped).T


def finish(me, pieces):
    return pl.pallas_call(
        finish_kernel,
        in_specs=[SCALARS] + [WHOLE] * NY,
        out_specs=WHOLE,
        out_shape=jax.ShapeDtypeStruct((LEVELS, ROWS, BLOCK), F32),
        scratch_shapes=[pltpu.VMEM((LEVELS, BLOCK, ROWS), F32)],
        compiler_params=PARAMS,
        name="finish",
    )(me, *pieces)


def per_device(codes, scales, factors, upstream):
    rows, wide = codes.shape
    blocks = 2 * NZ
    chunk = wide // blocks
    side, my_z, my_core, my_y = (lax.axis_index(name) for name in ("x0", "z", "core", "y"))
    first = (((lax.axis_index("x1") * 2 + side) * NZ + my_z) * 2 + my_core) * rows
    me = jnp.stack([my_y, my_z, my_core, side, first]).astype(jnp.int32)

    got = lax.all_to_all(pack(me, upstream, factors), ("z", "core"), 0, 0)
    mine, mixing = got[:, :chunk], got[:, chunk:]
    base = codes.astype(F32).reshape(rows, wide // rows, rows) * scales[0][None, :, None]
    base = base.reshape(rows, wide).astype(BF).T.reshape(blocks, chunk, rows)
    base = lax.all_to_all(base, ("z", "core"), 0, 0)
    theirs = lax.ppermute(mine, "x0", flips(2))

    partner = lax.ppermute(mixing[..., :BLOCK], "x0", flips(2))
    beside = jnp.where(my_y == NY - 1, partner, mixing[..., BLOCK:])
    mixing = jnp.concatenate([mixing[..., :BLOCK], beside], axis=2)
    near = jnp.stack([mixing] + [lax.ppermute(mixing, "y", flips(NY, k)) for k in range(1, NY)])
    dense = expand(me, near, lax.ppermute(near, "core", flips(2)))
    grads = grad_chain(dense, mine, theirs)
    own, away = scores(me, base, dense, grads, mine, theirs)

    pieces = core_sum(me, own, lax.ppermute(away, "core", flips(2)))
    total = pieces[0].astype(F32)
    for k in range(1, NY):
        total = total + lax.ppermute(pieces[k], "y", flips(NY, k)).astype(F32)
    total = total.astype(BF)
    far = lax.ppermute(total[:, TOP], "x0", flips(2))
    last = jnp.where(my_y < NY // 2, total[:, TOP], far)
    total = jnp.concatenate([total[:, :TOP], last[:, None]], axis=1)
    total = jnp.sum(lax.all_to_all(total, "z", 0, 0).astype(F32), axis=0)
    total = total + lax.ppermute(total, "zh", flips(2))
    return finish(me, [total] + [lax.ppermute(total, "y", flips(NY, k)) for k in range(1, NY)])


def solution(mesh):
    fsdp, col = mesh.devices.shape
    names = ("x1", "x0", "z", "core", "zh", "y")
    fine = Mesh(mesh.devices.reshape(fsdp // (4 * NZ), 2, NZ, 2, col // NY, NY), names)
    rows, cols = ("x1", "x0", "z", "core"), ("zh", "y")
    return jax.shard_map(
        per_device,
        mesh=fine,
        in_specs=(P(rows, cols), P(rows, cols), P(None, rows, None), P(rows, cols)),
        out_specs=P(None, rows, None),
        check_vma=False,
    )
```

```python
import functools

import jax
import jax.numpy as jnp
from jax import lax
from jax.experimental import pallas as pl
from jax.experimental.pallas import tpu as pltpu
from jax.sharding import Mesh
from jax.sharding import PartitionSpec as P

BF = jnp.bfloat16
F32 = jnp.float32
HALF = 32
BLOCK = 2 * HALF
ROWS = 128
LEVELS = 7
TOP = LEVELS - 1
NZ = 8
NY = 4
SLICE = BLOCK // NY
NAMES = ("x1", "x0", "z", "core", "zh", "y")
PARAMS = pltpu.CompilerParams(vmem_limit_bytes=16 * 2**20)
WHOLE = pl.BlockSpec(memory_space=pltpu.VMEM)
SCALARS = pl.BlockSpec(memory_space=pltpu.SMEM)


class Place:
    def __init__(self, me):
        index = me[0]
        self.y, self.core, self.z, self.x0 = index & 3, index >> 3 & 1, index >> 4 & 7, index >> 7 & 1
        self.first_row = (index >> 3) * ROWS


def dot(a, b):
    return lax.dot_general(a, b, (((1,), (0,)), ((), ())), preferred_element_type=F32)


def dot_nt(a, b):
    return lax.dot_general(a, b, (((1,), (1,)), ((), ())), preferred_element_type=F32)


def iota(shape, dim):
    return lax.broadcasted_iota(jnp.int32, shape, dim)


def flips(count, distance=1):
    return [(i, i ^ distance) for i in range(count)]


def units(level):
    if level == 2:
        return [[(2 * z, 2 * z + 1)] for z in range(NZ)]
    if level < 2 or level == TOP:
        return [[(2 * z, None), (2 * z + 1, None)] for z in range(NZ)]
    bit = level - 3
    lows = [z for z in range(NZ) if not z >> bit & 1]
    return [[(2 * z + c, 2 * (z | 1 << bit) + c) for c in range(2)] for z in lows]


def pack_kernel(me, upstream, factors, out):
    chunk = out.shape[1] - BLOCK
    for t in range(upstream.shape[1] // ROWS):
        turned = upstream[:, t * ROWS : (t + 1) * ROWS].T
        start, end = t * ROWS, (t + 1) * ROWS
        while start < end:
            block, at = start // chunk, start % chunk
            size = min(end - start, chunk - at)
            out[block, at : at + size] = turned[start - t * ROWS : start - t * ROWS + size]
            start += size
    place = Place(me)
    row = place.first_row + iota((BLOCK, ROWS), 1)
    sides = []
    for side in range(2):
        level = jnp.minimum(2 * place.y + side, TOP)
        pick = lax.shift_right_logical(row, level + 5) % 2 * HALF + row % HALF
        sides.append((iota((BLOCK, ROWS), 0) == pick).astype(F32) + factors[level])
    tile = jnp.concatenate(sides, axis=0).T.astype(BF)
    for block in range(out.shape[0]):
        half = block % 2 * BLOCK
        out[block, chunk:] = tile[half : half + BLOCK]


def pack(me, upstream, factors):
    rows, wide = upstream.shape
    return pl.pallas_call(
        pack_kernel,
        in_specs=[SCALARS, WHOLE, WHOLE],
        out_specs=WHOLE,
        out_shape=jax.ShapeDtypeStruct((2 * NZ, wide // (2 * NZ) + BLOCK, rows), BF),
        compiler_params=PARAMS,
        name="pack",
    )(me, upstream, factors)


def stack_kernel(me, *refs):
    *parts, _, out, top = refs
    place = Place(me)
    for k, part in enumerate(parts):
        out[k] = part[...]
    which = jnp.bitwise_xor(place.y, NY - 1)
    top[...] = out[which]


def stack(me, parts, after):
    return pl.pallas_call(
        stack_kernel,
        in_specs=[SCALARS] + [WHOLE] * NY + [pl.BlockSpec(memory_space=pl.ANY)],
        out_specs=[WHOLE] * 2,
        out_shape=[jax.ShapeDtypeStruct((NY,) + parts[0].shape, BF), jax.ShapeDtypeStruct(parts[0].shape, BF)],
        compiler_params=PARAMS,
        name="stack",
    )(me, *parts, after)


def expand_kernel(me, near, away, partner_near, partner_away, dense):
    place = Place(me)

    def run(level):
        width = ROWS if level < 2 else 2 * ROWS
        src, col = iota((ROWS, width), 0), iota((ROWS, width), 1)
        lane = level % 2 * BLOCK
        if level == 0:
            pick = src == lane + col % BLOCK
        elif level == 1:
            pick = src == lane + col // BLOCK * HALF + col % HALF
        elif level < TOP:
            pick = src == lane + col // ROWS * HALF + col % HALF
        else:
            pick = src == HALF * place.x0 + col % HALF
        pick = pick.astype(F32).astype(BF)
        which = jnp.bitwise_xor(place.y, level // 2)
        for c, (ref, partner) in enumerate(((near, partner_near), (away, partner_away))):
            at = pl.multiple_of(jnp.bitwise_xor(place.core, c) * BLOCK, BLOCK)
            row, col = at + iota((BLOCK, width), 0), iota((BLOCK, width), 1)
            if level == 0:
                keep = row // BLOCK == col // BLOCK
            elif level == 1:
                keep = (row // HALF) % 2 == (col // HALF) % 2
            else:
                keep = row // HALF == (col // HALF) % 4
            for block in range(2 * NZ):
                if level == TOP:
                    full = jnp.concatenate([dot(ref[which, block], pick[:, :ROWS]), dot(partner[block], pick[:, ROWS:])], axis=1)
                else:
                    full = dot(ref[which, block], pick)
                dense[0, block, pl.ds(at, BLOCK), :width] = jnp.where(keep, full, 0.0).astype(BF)

    for level in range(LEVELS):
        pl.when(pl.program_id(0) == level)(functools.partial(run, level))


def expand(me, near, away, partner_near, partner_away):
    shape = (2 * NZ, ROWS, 2 * ROWS)
    return pl.pallas_call(
        expand_kernel,
        grid=(LEVELS,),
        in_specs=[SCALARS] + [WHOLE] * 4,
        out_specs=pl.BlockSpec((1,) + shape, lambda s: (s, 0, 0, 0)),
        out_shape=jax.ShapeDtypeStruct((LEVELS,) + shape, BF),
        compiler_params=PARAMS,
        name="expand",
    )(me, near, away, partner_near, partner_away)


def grad_kernel(dense, mine, theirs, grads, state):
    def run(level):
        for unit in units(level):
            for lo, hi in unit:
                if level == TOP:
                    both = jnp.concatenate([mine[lo], theirs[lo]], axis=1)
                    full = jnp.concatenate([dense[0, lo, :, :ROWS], dense[0, lo, :, ROWS:]], axis=0)
                elif level == 1:
                    both, full = state[lo], dense[0, lo, :, :ROWS]
                else:
                    both = jnp.concatenate([state[lo], state[hi]], axis=1)
                    full = jnp.concatenate([dense[0, lo], dense[0, hi]], axis=0)
                out = dot(both, full).astype(BF)
                grads[0, lo] = out[:, :ROWS]
                if level > 1:
                    state[lo] = out[:, :ROWS]
                if hi is not None:
                    grads[0, hi] = out[:, ROWS:]
                    state[hi] = out[:, ROWS:]

    for s in range(TOP):
        pl.when(pl.program_id(0) == s)(functools.partial(run, TOP - s))


def grad_chain(dense, mine, theirs):
    blocks, wide, rows = mine.shape
    return pl.pallas_call(
        grad_kernel,
        grid=(TOP,),
        in_specs=[pl.BlockSpec((1, blocks, rows, 2 * rows), lambda s: (TOP - s, 0, 0, 0)), WHOLE, WHOLE],
        out_specs=pl.BlockSpec((1, blocks, wide, rows), lambda s: (TOP - 1 - s, 0, 0, 0)),
        out_shape=jax.ShapeDtypeStruct((TOP, blocks, wide, rows), BF),
        scratch_shapes=[pltpu.VMEM((blocks, wide, rows), BF)],
        compiler_params=PARAMS,
        name="grad_chain",
    )(dense, mine, theirs)


def fold(quad):
    lane = iota((HALF, ROWS), 1) // HALF
    out = quad[:HALF]
    for q in range(1, 4):
        out = jnp.where(lane == q, quad[q * HALF : (q + 1) * HALF], out)
    return out


def score_kernel(me, base, dense, grads, mine, theirs, own, away, state):
    first_core = Place(me).core == 0

    def store(z, parts):
        zero, one = parts
        mine_, other = jnp.where(first_core, zero, one), jnp.where(first_core, one, zero)
        for y in range(NY):
            own[y, z, 0] = mine_[y * SLICE : (y + 1) * SLICE].astype(BF)
            away[y, z, 0] = other[y * SLICE : (y + 1) * SLICE].astype(BF)

    def run(level):
        if level == 0:
            eye = (iota((ROWS, ROWS), 0) == iota((ROWS, ROWS), 1)).astype(F32).astype(BF)
        for unit in units(level):
            parts = {}
            for lo, hi in unit:
                if level == 0:
                    x = dot_nt(eye, base[lo]).astype(BF)
                elif hi is None:
                    x = state[lo]
                else:
                    x = jnp.concatenate([state[lo], state[hi]], axis=0)
                if level == TOP:
                    g = jnp.concatenate([mine[lo], theirs[lo]], axis=1)
                elif hi is None:
                    g = grads[0, lo]
                else:
                    g = jnp.concatenate([grads[0, lo], grads[0, hi]], axis=1)
                quad = dot(x, g)
                if level == 0:
                    parts[lo] = jnp.where(iota((BLOCK, ROWS), 1) < BLOCK, quad[:BLOCK], quad[BLOCK:])
                elif level == 1:
                    even = (iota((HALF, ROWS), 1) // HALF) % 2 == 0
                    rows = [quad[q * HALF : (q + 1) * HALF] for q in range(4)]
                    parts[lo] = jnp.concatenate([jnp.where(even, rows[0], rows[1]), jnp.where(even, rows[2], rows[3])], axis=0)
                elif level == TOP:
                    parts[lo] = jnp.concatenate([fold(quad[:, :ROWS]), fold(quad[:, ROWS:])], axis=0)
                else:
                    for b, at in ((lo, slice(0, ROWS)), (hi, slice(ROWS, 2 * ROWS))):
                        parts[b] = jnp.concatenate([fold(quad[:ROWS, at]), fold(quad[ROWS:, at])], axis=0)
                if level < 2:
                    state[lo] = dot(dense[0, lo, :, :ROWS], x).astype(BF)
                elif level < TOP:
                    full = jnp.concatenate([dense[0, lo], dense[0, hi]], axis=0)
                    out = dot(full, x).astype(BF)
                    state[lo], state[hi] = out[:ROWS], out[ROWS:]
            for z in sorted({b // 2 for b in parts}):
                store(z, (parts[2 * z], parts[2 * z + 1]))

    for level in range(LEVELS):
        pl.when(pl.program_id(0) == level)(functools.partial(run, level))


def scores(me, base, dense, grads, mine, theirs):
    blocks, wide, rows = base.shape
    shape = (NY, NZ, LEVELS, SLICE, rows)
    out_spec = pl.BlockSpec((NY, NZ, 1, SLICE, rows), lambda s: (0, 0, s, 0, 0))
    return pl.pallas_call(
        score_kernel,
        grid=(LEVELS,),
        in_specs=[
            SCALARS,
            WHOLE,
            pl.BlockSpec((1, blocks, rows, 2 * rows), lambda s: (jnp.minimum(s, TOP - 1), 0, 0, 0)),
            pl.BlockSpec((1, blocks, wide, rows), lambda s: (jnp.minimum(s, TOP - 1), 0, 0, 0)),
            WHOLE,
            WHOLE,
        ],
        out_specs=[out_spec, out_spec],
        out_shape=[jax.ShapeDtypeStruct(shape, BF)] * 2,
        scratch_shapes=[pltpu.VMEM((blocks, rows, wide), BF)],
        compiler_params=PARAMS,
        name="scores",
    )(me, base, dense, grads, mine, theirs)


def call(kernel, shape, *args):
    return pl.pallas_call(
        kernel,
        in_specs=[SCALARS] + [WHOLE] * (len(args) - 1),
        out_specs=WHOLE,
        out_shape=shape,
        compiler_params=PARAMS,
        name=kernel.__name__,
    )(*args)


def core_sum(me, own, got, out):
    for y in range(NY):
        out[y] = (own[y].astype(F32) + got[y].astype(F32)).astype(BF)


def copies_of_sum(me, parts, out):
    total = parts[0].astype(F32)
    for k in range(1, parts.shape[0]):
        total = total + parts[k].astype(F32)
    for k in range(out.shape[0]):
        out[k] = total.astype(out.dtype)


def finish(me, slices, out):
    my_x = Place(me).x0
    own, other = my_x * NY, (1 - my_x) * NY
    for y in range(NY):
        at = slice(y * SLICE, (y + 1) * SLICE)
        out[:TOP, at] = slices[own + y, :TOP].astype(F32)
    near = [slices[own + y, TOP].astype(F32) for y in range(NY // 2)]
    far = [slices[other + y, TOP].astype(F32) for y in range(NY // 2, NY)]
    for h, (even, odd) in enumerate(((near, far), (far, near))):
        for y in range(NY // 2):
            at = h * HALF + y * SLICE
            out[TOP, at : at + SLICE] = jnp.where(my_x == 0, even[y], odd[y])


def per_device(codes, scales, factors, upstream):
    rows, wide = codes.shape
    blocks = 2 * NZ
    chunk = wide // blocks
    me = lax.axis_index(NAMES).astype(jnp.int32).reshape(1)

    got = lax.all_to_all(pack(me, upstream, factors.transpose(0, 2, 1)), ("z", "core"), 0, 0)
    mine, mixing = got[:, :chunk], got[:, chunk:]
    base = codes.astype(F32).reshape(rows, wide // rows, rows) * scales[0][None, :, None]
    base = base.reshape(rows, wide).astype(BF).T.reshape(blocks, chunk, rows)
    base = lax.all_to_all(base, ("z", "core"), 0, 0)
    theirs = lax.ppermute(mine, "x0", flips(2))

    near = [mixing] + [lax.ppermute(mixing, "y", flips(NY, k)) for k in range(1, NY)]
    near, top = stack(me, near, theirs)
    away = lax.ppermute(near, "core", flips(2))
    partner_near = lax.ppermute(top, "x0", flips(2))
    partner_away = lax.ppermute(top, ("x0", "core"), flips(4, 3))
    dense = expand(me, near, away, partner_near, partner_away)
    grads = grad_chain(dense, mine, theirs)
    own, away = scores(me, base, dense, grads, mine, theirs)

    part = (LEVELS, SLICE, rows)
    total = call(core_sum, jax.ShapeDtypeStruct(own.shape, BF), me, own, lax.ppermute(away, "core", flips(2)))
    total = lax.all_to_all(total, "y", 0, 0)
    total = call(copies_of_sum, jax.ShapeDtypeStruct((2, NZ) + part, BF), me, total)
    total = lax.all_to_all(total.reshape((2 * NZ,) + part), ("zh", "z"), 0, 0)
    total = call(copies_of_sum, jax.ShapeDtypeStruct((2 * NY,) + part, BF), me, total)
    total = lax.all_to_all(total, ("x0", "y"), 0, 0)
    total = call(finish, jax.ShapeDtypeStruct((LEVELS, BLOCK, rows), F32), me, total)
    return total.transpose(0, 2, 1)


def solution(mesh):
    fsdp, col = mesh.devices.shape
    fine = Mesh(mesh.devices.reshape(fsdp // (4 * NZ), 2, NZ, 2, col // NY, NY), NAMES)
    rows, cols = ("x1", "x0", "z", "core"), ("zh", "y")
    return jax.shard_map(
        per_device,
        mesh=fine,
        in_specs=(P(rows, cols), P(rows, cols), P(None, rows, None), P(rows, cols)),
        out_specs=P(None, rows, None),
        check_vma=False,
    )
```

```python
import functools

import jax
import jax.numpy as jnp
from jax import lax
from jax.experimental import pallas as pl
from jax.experimental.pallas import tpu as pltpu
from jax.sharding import Mesh
from jax.sharding import PartitionSpec as P

BF = jnp.bfloat16
F32 = jnp.float32
HALF = 32
BLOCK = 2 * HALF
ROWS = 128
LEVELS = 7
TOP = LEVELS - 1
NZ = 8
NY = 4
SLICE = BLOCK // NY
NAMES = ("x1", "x0", "z", "core", "zh", "y")
PARAMS = pltpu.CompilerParams(vmem_limit_bytes=16 * 2**20)
WHOLE = pl.BlockSpec(memory_space=pltpu.VMEM)
SCALARS = pl.BlockSpec(memory_space=pltpu.SMEM)


class Place:
    def __init__(self, me):
        index = me[0]
        self.y, self.core, self.z, self.x0 = index & 3, index >> 3 & 1, index >> 4 & 7, index >> 7 & 1
        self.first_row = (index >> 3) * ROWS


def dot(a, b):
    return lax.dot_general(a, b, (((1,), (0,)), ((), ())), preferred_element_type=F32)


def dot_nt(a, b):
    return lax.dot_general(a, b, (((1,), (1,)), ((), ())), preferred_element_type=F32)


def iota(shape, dim):
    return lax.broadcasted_iota(jnp.int32, shape, dim)


def flips(count, distance=1):
    return [(i, i ^ distance) for i in range(count)]


def units(level):
    if level == 2:
        return [[(2 * z, 2 * z + 1)] for z in range(NZ)]
    if level < 2 or level == TOP:
        return [[(2 * z, None), (2 * z + 1, None)] for z in range(NZ)]
    bit = level - 3
    lows = [z for z in range(NZ) if not z >> bit & 1]
    return [[(2 * z + c, 2 * (z | 1 << bit) + c) for c in range(2)] for z in lows]


def pack_kernel(me, upstream, factors, out):
    chunk = out.shape[1] - BLOCK
    for t in range(upstream.shape[1] // ROWS):
        turned = upstream[:, t * ROWS : (t + 1) * ROWS].T
        start, end = t * ROWS, (t + 1) * ROWS
        while start < end:
            block, at = start // chunk, start % chunk
            size = min(end - start, chunk - at)
            out[block, at : at + size] = turned[start - t * ROWS : start - t * ROWS + size]
            start += size
    place = Place(me)
    row = place.first_row + iota((BLOCK, ROWS), 1)
    sides = []
    for side in range(2):
        level = jnp.minimum(2 * place.y + side, TOP)
        pick = lax.shift_right_logical(row, level + 5) % 2 * HALF + row % HALF
        sides.append((iota((BLOCK, ROWS), 0) == pick).astype(F32) + factors[level])
    tile = jnp.concatenate(sides, axis=0).T.astype(BF)
    for block in range(out.shape[0]):
        half = block % 2 * BLOCK
        out[block, chunk:] = tile[half : half + BLOCK]


def pack(me, upstream, factors):
    rows, wide = upstream.shape
    return pl.pallas_call(
        pack_kernel,
        in_specs=[SCALARS, WHOLE, WHOLE],
        out_specs=WHOLE,
        out_shape=jax.ShapeDtypeStruct((2 * NZ, wide // (2 * NZ) + BLOCK, rows), BF),
        compiler_params=PARAMS,
        name="pack",
    )(me, upstream, factors)


def stack_kernel(me, *refs):
    *parts, _, out, top = refs
    place = Place(me)
    for k, part in enumerate(parts):
        out[k] = part[...]
    which = jnp.bitwise_xor(place.y, NY - 1)
    src, col = iota((ROWS, ROWS), 0), iota((ROWS, ROWS), 1)
    picks = []
    for j in range(4):
        pick = (col // HALF == j) & (src == HALF * (1 - place.x0) + col % HALF)
        picks.append(pick.astype(F32).astype(BF))
    for k in range(top.shape[0]):
        packed = dot(out[which, 4 * k], picks[0])
        for j in range(1, 4):
            packed = packed + dot(out[which, 4 * k + j], picks[j])
        top[k] = packed.astype(BF)


def stack(me, parts, after):
    blocks, rows, wide = parts[0].shape
    return pl.pallas_call(
        stack_kernel,
        in_specs=[SCALARS] + [WHOLE] * NY + [pl.BlockSpec(memory_space=pl.ANY)],
        out_specs=[WHOLE] * 2,
        out_shape=[
            jax.ShapeDtypeStruct((NY, blocks, rows, wide), BF),
            jax.ShapeDtypeStruct((blocks // 4, rows, wide), BF),
        ],
        compiler_params=PARAMS,
        name="stack",
    )(me, *parts, after)


def spreader(level, my_x):
    width = 2 * ROWS if 2 <= level < TOP else ROWS
    src, col = iota((ROWS, width), 0), iota((ROWS, width), 1)
    lane = level % 2 * BLOCK

    def keep(first):
        row, column = first + iota((BLOCK, width), 0), iota((BLOCK, width), 1)
        if level == 0:
            return row // BLOCK == column // BLOCK
        parts = 2 if level == 1 else 4
        return (row // HALF) % parts == (column // HALF) % parts

    if level == 0:
        picks = [src == lane + col % BLOCK]
    elif level == 1:
        picks = [src == lane + col // BLOCK * HALF + col % HALF]
    elif level < TOP:
        picks = [src == lane + col // ROWS * HALF + col % HALF]
    else:
        picks = [src == HALF * my_x + col % HALF] + [src == HALF * j + col % HALF for j in range(4)]
    return [pick.astype(F32).astype(BF) for pick in picks], keep


def expand_kernel(me, near, away, partner_near, partner_away, _, *dense):
    place = Place(me)
    for level in reversed(range(LEVELS)):
        picks, keep = spreader(level, place.x0)
        which = jnp.bitwise_xor(place.y, level // 2)
        for c, (ref, partner) in enumerate(((near, partner_near), (away, partner_away))):
            first = jnp.bitwise_xor(place.core, c) * BLOCK
            at = pl.ds(pl.multiple_of(first, BLOCK), BLOCK)
            mask = keep(first)
            for block in range(2 * NZ):
                full = jnp.where(mask, dot(ref[which, block], picks[0]), 0.0).astype(BF)
                dense[level][block, at, : full.shape[1]] = full
                if level == TOP:
                    far = dot(partner[block // 4], picks[1 + block % 4])
                    dense[level][block, at, ROWS:] = jnp.where(mask, far, 0.0).astype(BF)


def expand(me, near, away, partner_near, partner_away, after):
    narrow, wide = (2 * NZ, ROWS, ROWS), (2 * NZ, ROWS, 2 * ROWS)
    return pl.pallas_call(
        expand_kernel,
        in_specs=[SCALARS] + [WHOLE] * 4 + [pl.BlockSpec(memory_space=pl.ANY)],
        out_specs=[WHOLE] * LEVELS,
        out_shape=[jax.ShapeDtypeStruct(narrow if level < 2 else wide, BF) for level in range(LEVELS)],
        compiler_params=PARAMS,
        name="expand",
    )(me, near, away, partner_near, partner_away, after)


def grad_kernel(*refs):
    dense, mine, theirs, grads = refs[:TOP], refs[TOP], refs[TOP + 1], refs[TOP + 2 :]
    for level in range(TOP, 0, -1):
        mix, above, out_ref = dense[level - 1], grads[level] if level < TOP else None, grads[level - 1]
        for unit in units(level):
            for lo, hi in unit:
                if level == TOP:
                    both = jnp.concatenate([mine[lo], theirs[lo]], axis=1)
                    full = jnp.concatenate([mix[lo, :, :ROWS], mix[lo, :, ROWS:]], axis=0)
                elif level == 1:
                    both, full = above[lo], mix[lo]
                else:
                    both = jnp.concatenate([above[lo], above[hi]], axis=1)
                    full = jnp.concatenate([mix[lo], mix[hi]], axis=0)
                out = dot(both, full).astype(BF)
                out_ref[lo] = out[:, :ROWS]
                if hi is not None:
                    out_ref[hi] = out[:, ROWS:]


def grad_chain(dense, mine, theirs):
    return pl.pallas_call(
        grad_kernel,
        in_specs=[WHOLE] * (TOP + 2),
        out_specs=[WHOLE] * TOP,
        out_shape=[jax.ShapeDtypeStruct(mine.shape, BF)] * TOP,
        compiler_params=PARAMS,
        name="grad_chain",
    )(*dense, mine, theirs)


def fold(quad):
    lane = iota((HALF, ROWS), 1) // HALF
    out = quad[:HALF]
    for q in range(1, 4):
        out = jnp.where(lane == q, quad[q * HALF : (q + 1) * HALF], out)
    return out


def score_kernel(me, base, *refs):
    dense, grads = refs[:TOP], refs[TOP : 2 * TOP]
    mine, theirs, own, away, *states = refs[2 * TOP :]
    first_core = Place(me).core == 0

    def store(level, z, parts):
        zero, one = parts
        mine_, other = jnp.where(first_core, zero, one), jnp.where(first_core, one, zero)
        for y in range(NY):
            own[y, z, level] = mine_[y * SLICE : (y + 1) * SLICE].astype(BF)
            away[y, z, level] = other[y * SLICE : (y + 1) * SLICE].astype(BF)

    eye = (iota((ROWS, ROWS), 0) == iota((ROWS, ROWS), 1)).astype(F32).astype(BF)
    for level in range(LEVELS):
        state, after = states[level % 2], states[1 - level % 2]
        for unit in units(level):
            parts = {}
            for lo, hi in unit:
                if level == 0:
                    x = dot_nt(eye, base[lo]).astype(BF)
                elif hi is None:
                    x = state[lo]
                else:
                    x = jnp.concatenate([state[lo], state[hi]], axis=0)
                if level == TOP:
                    g = jnp.concatenate([mine[lo], theirs[lo]], axis=1)
                elif hi is None:
                    g = grads[level][lo]
                else:
                    g = jnp.concatenate([grads[level][lo], grads[level][hi]], axis=1)
                if level < 2:
                    after[lo] = dot(dense[level][lo], x).astype(BF)
                elif level < TOP:
                    full = jnp.concatenate([dense[level][lo], dense[level][hi]], axis=0)
                    out = dot(full, x).astype(BF)
                    after[lo], after[hi] = out[:ROWS], out[ROWS:]
                quad = dot(x, g)
                if level == 0:
                    parts[lo] = jnp.where(iota((BLOCK, ROWS), 1) < BLOCK, quad[:BLOCK], quad[BLOCK:])
                elif level == 1:
                    even = (iota((HALF, ROWS), 1) // HALF) % 2 == 0
                    rows = [quad[q * HALF : (q + 1) * HALF] for q in range(4)]
                    parts[lo] = jnp.concatenate([jnp.where(even, rows[0], rows[1]), jnp.where(even, rows[2], rows[3])], axis=0)
                elif level == TOP:
                    parts[lo] = jnp.concatenate([fold(quad[:, :ROWS]), fold(quad[:, ROWS:])], axis=0)
                else:
                    for b, at in ((lo, slice(0, ROWS)), (hi, slice(ROWS, 2 * ROWS))):
                        parts[b] = jnp.concatenate([fold(quad[:ROWS, at]), fold(quad[ROWS:, at])], axis=0)
            for z in sorted({b // 2 for b in parts}):
                store(level, z, (parts[2 * z], parts[2 * z + 1]))


def scores(me, base, dense, grads, mine, theirs):
    blocks, wide, rows = base.shape
    shape = (NY, NZ, LEVELS, SLICE, rows)
    return pl.pallas_call(
        score_kernel,
        in_specs=[SCALARS] + [WHOLE] * (2 * TOP + 3),
        out_specs=[WHOLE] * 2,
        out_shape=[jax.ShapeDtypeStruct(shape, BF)] * 2,
        scratch_shapes=[pltpu.VMEM((blocks, rows, wide), BF)] * 2,
        compiler_params=PARAMS,
        name="scores",
    )(me, base, *dense, *grads, mine, theirs)


def call(kernel, shape, *args):
    return pl.pallas_call(
        kernel,
        in_specs=[SCALARS] + [WHOLE] * (len(args) - 1),
        out_specs=WHOLE,
        out_shape=shape,
        compiler_params=PARAMS,
        name=kernel.__name__,
    )(*args)


def core_sum(me, own, got, out):
    for y in range(NY):
        out[y] = (own[y].astype(F32) + got[y].astype(F32)).astype(BF)


def copies_of_sum(me, parts, out):
    total = parts[0].astype(F32)
    for k in range(1, parts.shape[0]):
        total = total + parts[k].astype(F32)
    for k in range(out.shape[0]):
        out[k] = total.astype(out.dtype)


def finish(me, slices, out):
    my_x = Place(me).x0
    own, other = my_x * NY, (1 - my_x) * NY
    for y in range(NY):
        at = slice(y * SLICE, (y + 1) * SLICE)
        out[:TOP, at] = slices[own + y, :TOP].astype(F32)
    near = [slices[own + y, TOP].astype(F32) for y in range(NY // 2)]
    far = [slices[other + y, TOP].astype(F32) for y in range(NY // 2, NY)]
    for h, (even, odd) in enumerate(((near, far), (far, near))):
        for y in range(NY // 2):
            at = h * HALF + y * SLICE
            out[TOP, at : at + SLICE] = jnp.where(my_x == 0, even[y], odd[y])


def per_device(codes, scales, factors, upstream):
    rows, wide = codes.shape
    blocks = 2 * NZ
    chunk = wide // blocks
    me = lax.axis_index(NAMES).astype(jnp.int32).reshape(1)

    got = lax.all_to_all(pack(me, upstream, factors.transpose(0, 2, 1)), ("z", "core"), 0, 0)
    mine, mixing = got[:, :chunk], got[:, chunk:]
    base = codes.astype(F32).reshape(rows, wide // rows, rows) * scales[0][None, :, None]
    base = base.reshape(rows, wide).astype(BF).T.reshape(blocks, chunk, rows)
    base = lax.all_to_all(base, ("z", "core"), 0, 0)
    theirs = lax.ppermute(mine, "x0", flips(2))

    near = [mixing] + [lax.ppermute(mixing, "y", flips(NY, k)) for k in range(1, NY)]
    near, top = stack(me, near, theirs)
    away = lax.ppermute(near, "core", flips(2))
    partner_near = lax.ppermute(top, "x0", flips(2))
    partner_away = lax.ppermute(top, ("x0", "core"), flips(4, 3))
    dense = expand(me, near, away, partner_near, partner_away, base)
    grads = grad_chain(dense[1:], mine, theirs)
    own, away = scores(me, base, dense[:TOP], grads, mine, theirs)

    part = (LEVELS, SLICE, rows)
    total = call(core_sum, jax.ShapeDtypeStruct(own.shape, BF), me, own, lax.ppermute(away, "core", flips(2)))
    total = lax.all_to_all(total, "y", 0, 0)
    total = call(copies_of_sum, jax.ShapeDtypeStruct((2, NZ) + part, BF), me, total)
    total = lax.all_to_all(total.reshape((2 * NZ,) + part), ("zh", "z"), 0, 0)
    total = call(copies_of_sum, jax.ShapeDtypeStruct((2 * NY,) + part, BF), me, total)
    total = lax.all_to_all(total, ("x0", "y"), 0, 0)
    total = call(finish, jax.ShapeDtypeStruct((LEVELS, BLOCK, rows), F32), me, total)
    return total.transpose(0, 2, 1)


def solution(mesh):
    fsdp, col = mesh.devices.shape
    fine = Mesh(mesh.devices.reshape(fsdp // (4 * NZ), 2, NZ, 2, col // NY, NY), NAMES)
    rows, cols = ("x1", "x0", "z", "core"), ("zh", "y")
    return jax.shard_map(
        per_device,
        mesh=fine,
        in_specs=(P(rows, cols), P(rows, cols), P(None, rows, None), P(rows, cols)),
        out_specs=P(None, rows, None),
        check_vma=False,
    )
```

```python
import functools

import jax
import jax.numpy as jnp
from jax import lax
from jax.experimental import pallas as pl
from jax.experimental.pallas import tpu as pltpu
from jax.sharding import Mesh
from jax.sharding import PartitionSpec as P

BF = jnp.bfloat16
F32 = jnp.float32
HALF = 32
BLOCK = 2 * HALF
ROWS = 128
LEVELS = 7
TOP = LEVELS - 1
NZ = 8
NY = 4
SLICE = BLOCK // NY
NAMES = ("x1", "x0", "z", "core", "zh", "y")
PARAMS = pltpu.CompilerParams(vmem_limit_bytes=16 * 2**20)
WHOLE = pl.BlockSpec(memory_space=pltpu.VMEM)
SCALARS = pl.BlockSpec(memory_space=pltpu.SMEM)


class Place:
    def __init__(self, me):
        index = me[0]
        self.y, self.core, self.z, self.x0 = index & 3, index >> 3 & 1, index >> 4 & 7, index >> 7 & 1
        self.first_row = (index >> 3) * ROWS


def dot(a, b):
    return lax.dot_general(a, b, (((1,), (0,)), ((), ())), preferred_element_type=F32)


def dot_nt(a, b):
    return lax.dot_general(a, b, (((1,), (1,)), ((), ())), preferred_element_type=F32)


def iota(shape, dim):
    return lax.broadcasted_iota(jnp.int32, shape, dim)


def flips(count, distance=1):
    return [(i, i ^ distance) for i in range(count)]


def units(level):
    if level == 2:
        return [[(2 * z, 2 * z + 1)] for z in range(NZ)]
    if level < 2 or level == TOP:
        return [[(2 * z, None), (2 * z + 1, None)] for z in range(NZ)]
    bit = level - 3
    lows = [z for z in range(NZ) if not z >> bit & 1]
    return [[(2 * z + c, 2 * (z | 1 << bit) + c) for c in range(2)] for z in lows]


def pack_kernel(me, upstream, factors, out, wide, mix, turned, in_sems, mix_sem, out_sems):
    place = Place(me)
    blocks = turned.shape[0]
    chunk = turned.shape[1] - BLOCK
    tiles = wide.shape[1] // ROWS
    count = in_sems.shape[0]
    edges = [ROWS * (tiles * i // count) for i in range(count + 1)]
    loads = [
        pltpu.make_async_copy(upstream.at[:, lo:hi], wide.at[:, lo:hi], in_sems.at[i])
        for i, (lo, hi) in enumerate(zip(edges, edges[1:]))
    ]
    load_mix = pltpu.make_async_copy(factors, mix, mix_sem)
    load_mix.start()
    for load in loads:
        load.start()
    load_mix.wait()
    row = place.first_row + iota((BLOCK, ROWS), 1)
    sides = []
    for side in range(2):
        level = jnp.minimum(2 * place.y + side, TOP)
        pick = lax.shift_right_logical(row, level + 5) % 2 * HALF + row % HALF
        sides.append((iota((BLOCK, ROWS), 0) == pick).astype(F32) + mix[level])
    tile = jnp.concatenate(sides, axis=0).T.astype(BF)
    for block in range(blocks):
        half = block % 2 * BLOCK
        turned[block, chunk:] = tile[half : half + BLOCK]
    stores = []
    group = blocks // out_sems.shape[0]
    for t in range(tiles):
        if t * ROWS in edges:
            loads[edges.index(t * ROWS)].wait()
        columns = wide[:, t * ROWS : (t + 1) * ROWS].T
        start, end = t * ROWS, (t + 1) * ROWS
        while start < end:
            block, at = start // chunk, start % chunk
            size = min(end - start, chunk - at)
            turned[block, at : at + size] = columns[start - t * ROWS : start - t * ROWS + size]
            start += size
        while len(stores) < out_sems.shape[0] and end >= (len(stores) + 1) * group * chunk:
            at = slice(len(stores) * group, (len(stores) + 1) * group)
            stores.append(pltpu.make_async_copy(turned.at[at], out.at[at], out_sems.at[len(stores)]))
            stores[-1].start()
    for store in stores:
        store.wait()


def pack(me, upstream, factors):
    rows, wide = upstream.shape
    shape = (2 * NZ, wide // (2 * NZ) + BLOCK, rows)
    hbm = pl.BlockSpec(memory_space=pltpu.HBM)
    return pl.pallas_call(
        pack_kernel,
        in_specs=[SCALARS, hbm, hbm],
        out_specs=hbm,
        out_shape=jax.ShapeDtypeStruct(shape, BF),
        scratch_shapes=[
            pltpu.VMEM((rows, wide), BF),
            pltpu.VMEM(factors.shape, F32),
            pltpu.VMEM(shape, BF),
            pltpu.SemaphoreType.DMA((4,)),
            pltpu.SemaphoreType.DMA,
            pltpu.SemaphoreType.DMA((4,)),
        ],
        compiler_params=pltpu.CompilerParams(vmem_limit_bytes=58 * 2**20),
        name="pack",
    )(me, upstream, factors)


def stack_kernel(me, *refs):
    *parts, _, out, top = refs
    place = Place(me)
    for k, part in enumerate(parts):
        out[k] = part[...]
    which = jnp.bitwise_xor(place.y, NY - 1)
    src, col = iota((ROWS, ROWS), 0), iota((ROWS, ROWS), 1)
    picks = []
    for j in range(4):
        pick = (col // HALF == j) & (src == HALF * (1 - place.x0) + col % HALF)
        picks.append(pick.astype(F32).astype(BF))
    for k in range(top.shape[0]):
        packed = dot(out[which, 4 * k], picks[0])
        for j in range(1, 4):
            packed = packed + dot(out[which, 4 * k + j], picks[j])
        top[k] = packed.astype(BF)


def stack(me, parts, after):
    blocks, rows, wide = parts[0].shape
    return pl.pallas_call(
        stack_kernel,
        in_specs=[SCALARS] + [WHOLE] * NY + [pl.BlockSpec(memory_space=pl.ANY)],
        out_specs=[WHOLE] * 2,
        out_shape=[
            jax.ShapeDtypeStruct((NY, blocks, rows, wide), BF),
            jax.ShapeDtypeStruct((blocks // 4, rows, wide), BF),
        ],
        compiler_params=PARAMS,
        name="stack",
    )(me, *parts, after)


def spreader(level, my_x):
    width = 2 * ROWS if 2 <= level < TOP else ROWS
    src, col = iota((ROWS, width), 0), iota((ROWS, width), 1)
    lane = level % 2 * BLOCK
    parts = 2 if level == 1 else 4
    keep = (src // HALF) % parts == (col // HALF) % parts
    if level == 0:
        picks, keep = [src == lane + col % BLOCK], src // BLOCK == col // BLOCK
    elif level == 1:
        picks = [src == lane + col // BLOCK * HALF + col % HALF]
    elif level < TOP:
        picks = [src == lane + col // ROWS * HALF + col % HALF]
    else:
        picks = [src == HALF * my_x + col % HALF] + [src == HALF * j + col % HALF for j in range(4)]
    return [pick.astype(F32).astype(BF) for pick in picks], keep


def expand_kernel(me, near, away, partner_near, partner_away, _, *refs):
    dense, held, sems = refs[:LEVELS], refs[LEVELS:-1], refs[-1]
    place = Place(me)
    first_core = place.core == 0
    loads = [[] for _ in range(NY)]
    for j in reversed(range(NY)):
        for c, ref in enumerate((near, away)):
            loads[j].append(pltpu.make_async_copy(ref.at[jnp.bitwise_xor(place.y, j)], held[c].at[j], sems.at[j, c]))
        if j == NY - 1:
            for c, ref in enumerate((partner_near, partner_away)):
                loads[j].append(pltpu.make_async_copy(ref, held[2 + c], sems.at[NY, c]))
        for load in loads[j]:
            load.start()

    def rows(one, other):
        return jnp.concatenate([jnp.where(first_core, one, other), jnp.where(first_core, other, one)], axis=0)

    for level in reversed(range(LEVELS)):
        if level == TOP or level % 2:
            for load in loads[level // 2]:
                load.wait()
        picks, keep = spreader(level, place.x0)
        for block in range(2 * NZ):
            full = dot(rows(held[0][level // 2, block], held[1][level // 2, block]), picks[0])
            dense[level][block, :, : full.shape[1]] = jnp.where(keep, full, 0.0).astype(BF)
            if level == TOP:
                far = dot(rows(held[2][block // 4], held[3][block // 4]), picks[1 + block % 4])
                dense[level][block, :, ROWS:] = jnp.where(keep, far, 0.0).astype(BF)


def expand(me, near, away, partner_near, partner_away, after):
    narrow, wide = (2 * NZ, ROWS, ROWS), (2 * NZ, ROWS, 2 * ROWS)
    return pl.pallas_call(
        expand_kernel,
        in_specs=[SCALARS] + [pl.BlockSpec(memory_space=pl.ANY)] * 5,
        out_specs=[WHOLE] * LEVELS,
        out_shape=[jax.ShapeDtypeStruct(narrow if level < 2 else wide, BF) for level in range(LEVELS)],
        scratch_shapes=[pltpu.VMEM(near.shape, BF)] * 2
        + [pltpu.VMEM(partner_near.shape, BF)] * 2
        + [pltpu.SemaphoreType.DMA((NY + 1, 2))],
        compiler_params=PARAMS,
        name="expand",
    )(me, near, away, partner_near, partner_away, after)


def grad_kernel(*refs):
    dense, mine, theirs, grads = refs[:TOP], refs[TOP], refs[TOP + 1], refs[TOP + 2 :]
    for level in range(TOP, 0, -1):
        mix, above, out_ref = dense[level - 1], grads[level] if level < TOP else None, grads[level - 1]
        for unit in units(level):
            for lo, hi in unit:
                if level == TOP:
                    both = jnp.concatenate([mine[lo], theirs[lo]], axis=1)
                    full = jnp.concatenate([mix[lo, :, :ROWS], mix[lo, :, ROWS:]], axis=0)
                elif level == 1:
                    both, full = above[lo], mix[lo]
                else:
                    both = jnp.concatenate([above[lo], above[hi]], axis=1)
                    full = jnp.concatenate([mix[lo], mix[hi]], axis=0)
                out = dot(both, full).astype(BF)
                out_ref[lo] = out[:, :ROWS]
                if hi is not None:
                    out_ref[hi] = out[:, ROWS:]


def grad_chain(dense, mine, theirs):
    return pl.pallas_call(
        grad_kernel,
        in_specs=[WHOLE] * (TOP + 2),
        out_specs=[WHOLE] * TOP,
        out_shape=[jax.ShapeDtypeStruct(mine.shape, BF)] * TOP,
        compiler_params=PARAMS,
        name="grad_chain",
    )(*dense, mine, theirs)


def fold(quad):
    lane = iota((HALF, ROWS), 1) // HALF
    out = quad[:HALF]
    for q in range(1, 4):
        out = jnp.where(lane == q, quad[q * HALF : (q + 1) * HALF], out)
    return out


def score_kernel(me, base, *refs):
    dense, grads = refs[:TOP], refs[TOP : 2 * TOP]
    mine, theirs, own, away, *states = refs[2 * TOP :]
    first_core = Place(me).core == 0

    def store(level, z, parts):
        zero, one = parts
        mine_, other = jnp.where(first_core, zero, one), jnp.where(first_core, one, zero)
        for y in range(NY):
            own[y, z, level] = mine_[y * SLICE : (y + 1) * SLICE].astype(BF)
            away[y, z, level] = other[y * SLICE : (y + 1) * SLICE].astype(BF)

    eye = (iota((ROWS, ROWS), 0) == iota((ROWS, ROWS), 1)).astype(F32).astype(BF)
    for level in range(LEVELS):
        state, after = states[level % 2], states[1 - level % 2]
        for unit in units(level):
            parts = {}
            for lo, hi in unit:
                if level == 0:
                    x = dot_nt(eye, base[lo]).astype(BF)
                elif hi is None:
                    x = state[lo]
                else:
                    x = jnp.concatenate([state[lo], state[hi]], axis=0)
                if level == TOP:
                    g = jnp.concatenate([mine[lo], theirs[lo]], axis=1)
                elif hi is None:
                    g = grads[level][lo]
                else:
                    g = jnp.concatenate([grads[level][lo], grads[level][hi]], axis=1)
                if level < 2:
                    after[lo] = dot(dense[level][lo], x).astype(BF)
                elif level < TOP:
                    full = jnp.concatenate([dense[level][lo], dense[level][hi]], axis=0)
                    out = dot(full, x).astype(BF)
                    after[lo], after[hi] = out[:ROWS], out[ROWS:]
                quad = dot(x, g)
                if level == 0:
                    parts[lo] = jnp.where(iota((BLOCK, ROWS), 1) < BLOCK, quad[:BLOCK], quad[BLOCK:])
                elif level == 1:
                    even = (iota((HALF, ROWS), 1) // HALF) % 2 == 0
                    rows = [quad[q * HALF : (q + 1) * HALF] for q in range(4)]
                    parts[lo] = jnp.concatenate([jnp.where(even, rows[0], rows[1]), jnp.where(even, rows[2], rows[3])], axis=0)
                elif level == TOP:
                    parts[lo] = jnp.concatenate([fold(quad[:, :ROWS]), fold(quad[:, ROWS:])], axis=0)
                else:
                    for b, at in ((lo, slice(0, ROWS)), (hi, slice(ROWS, 2 * ROWS))):
                        parts[b] = jnp.concatenate([fold(quad[:ROWS, at]), fold(quad[ROWS:, at])], axis=0)
            for z in sorted({b // 2 for b in parts}):
                store(level, z, (parts[2 * z], parts[2 * z + 1]))


def scores(me, base, dense, grads, mine, theirs):
    blocks, wide, rows = base.shape
    shape = (NY, NZ, LEVELS, SLICE, rows)
    return pl.pallas_call(
        score_kernel,
        in_specs=[SCALARS] + [WHOLE] * (2 * TOP + 3),
        out_specs=[WHOLE] * 2,
        out_shape=[jax.ShapeDtypeStruct(shape, BF)] * 2,
        scratch_shapes=[pltpu.VMEM((blocks, rows, wide), BF)] * 2,
        compiler_params=PARAMS,
        name="scores",
    )(me, base, *dense, *grads, mine, theirs)


def call(kernel, shape, *args):
    return pl.pallas_call(
        kernel,
        in_specs=[SCALARS] + [WHOLE] * (len(args) - 1),
        out_specs=WHOLE,
        out_shape=shape,
        compiler_params=PARAMS,
        name=kernel.__name__,
    )(*args)


def core_sum(me, own, got, out):
    for y in range(NY):
        out[y] = (own[y].astype(F32) + got[y].astype(F32)).astype(BF)


def copies_of_sum(me, parts, out):
    total = parts[0].astype(F32)
    for k in range(1, parts.shape[0]):
        total = total + parts[k].astype(F32)
    for k in range(out.shape[0]):
        out[k] = total.astype(out.dtype)


def finish(me, slices, out):
    my_x = Place(me).x0
    own, other = my_x * NY, (1 - my_x) * NY
    for y in range(NY):
        at = slice(y * SLICE, (y + 1) * SLICE)
        out[:TOP, at] = slices[own + y, :TOP].astype(F32)
    near = [slices[own + y, TOP].astype(F32) for y in range(NY // 2)]
    far = [slices[other + y, TOP].astype(F32) for y in range(NY // 2, NY)]
    for h, (even, odd) in enumerate(((near, far), (far, near))):
        for y in range(NY // 2):
            at = h * HALF + y * SLICE
            out[TOP, at : at + SLICE] = jnp.where(my_x == 0, even[y], odd[y])


def per_device(codes, scales, factors, upstream):
    rows, wide = codes.shape
    blocks = 2 * NZ
    chunk = wide // blocks
    me = lax.axis_index(NAMES).astype(jnp.int32).reshape(1)

    got = lax.all_to_all(pack(me, upstream, factors.transpose(0, 2, 1)), ("z", "core"), 0, 0)
    mine, mixing = got[:, :chunk], got[:, chunk:]
    base = codes.astype(F32).reshape(rows, wide // rows, rows) * scales[0][None, :, None]
    base = base.reshape(rows, wide).astype(BF).T.reshape(blocks, chunk, rows)
    base = lax.all_to_all(base, ("z", "core"), 0, 0)
    theirs = lax.ppermute(mine, "x0", flips(2))

    near = [mixing] + [lax.ppermute(mixing, "y", flips(NY, k)) for k in range(1, NY)]
    near, top = stack(me, near, theirs)
    away = lax.ppermute(near, "core", flips(2))
    partner_near = lax.ppermute(top, "x0", flips(2))
    partner_away = lax.ppermute(top, ("x0", "core"), flips(4, 3))
    dense = expand(me, near, away, partner_near, partner_away, base)
    grads = grad_chain(dense[1:], mine, theirs)
    own, away = scores(me, base, dense[:TOP], grads, mine, theirs)

    part = (LEVELS, SLICE, rows)
    total = call(core_sum, jax.ShapeDtypeStruct(own.shape, BF), me, own, lax.ppermute(away, "core", flips(2)))
    total = lax.all_to_all(total, "y", 0, 0)
    total = call(copies_of_sum, jax.ShapeDtypeStruct((2, NZ) + part, BF), me, total)
    total = lax.all_to_all(total.reshape((2 * NZ,) + part), ("zh", "z"), 0, 0)
    total = call(copies_of_sum, jax.ShapeDtypeStruct((2 * NY,) + part, BF), me, total)
    total = lax.all_to_all(total, ("x0", "y"), 0, 0)
    total = call(finish, jax.ShapeDtypeStruct((LEVELS, BLOCK, rows), F32), me, total)
    return total.transpose(0, 2, 1)


def solution(mesh):
    fsdp, col = mesh.devices.shape
    fine = Mesh(mesh.devices.reshape(fsdp // (4 * NZ), 2, NZ, 2, col // NY, NY), NAMES)
    rows, cols = ("x1", "x0", "z", "core"), ("zh", "y")
    return jax.shard_map(
        per_device,
        mesh=fine,
        in_specs=(P(rows, cols), P(rows, cols), P(None, rows, None), P(rows, cols)),
        out_specs=P(None, rows, None),
        check_vma=False,
    )
```

```python
import functools

import jax
import jax.numpy as jnp
from jax import lax
from jax.experimental import pallas as pl
from jax.experimental.pallas import tpu as pltpu
from jax.sharding import Mesh
from jax.sharding import PartitionSpec as P

BF = jnp.bfloat16
F32 = jnp.float32
HALF = 32
BLOCK = 2 * HALF
ROWS = 128
LEVELS = 7
TOP = LEVELS - 1
NZ = 8
NY = 4
SLICE = BLOCK // NY
NAMES = ("x1", "x0", "z", "core", "zh", "y")
PARAMS = pltpu.CompilerParams(vmem_limit_bytes=16 * 2**20)
WHOLE = pl.BlockSpec(memory_space=pltpu.VMEM)
SCALARS = pl.BlockSpec(memory_space=pltpu.SMEM)


class Place:
    def __init__(self, me):
        index = me[0]
        self.y, self.core, self.z, self.x0 = index & 3, index >> 3 & 1, index >> 4 & 7, index >> 7 & 1
        self.first_row = (index >> 3) * ROWS


def dot(a, b):
    return lax.dot_general(a, b, (((1,), (0,)), ((), ())), preferred_element_type=F32)


def dot_nt(a, b):
    return lax.dot_general(a, b, (((1,), (1,)), ((), ())), preferred_element_type=F32)


def iota(shape, dim):
    return lax.broadcasted_iota(jnp.int32, shape, dim)


def flips(count, distance=1):
    return [(i, i ^ distance) for i in range(count)]


def units(level):
    if level == 2:
        return [[(2 * z, 2 * z + 1)] for z in range(NZ)]
    if level < 2 or level == TOP:
        return [[(2 * z, None), (2 * z + 1, None)] for z in range(NZ)]
    bit = level - 3
    lows = [z for z in range(NZ) if not z >> bit & 1]
    return [[(2 * z + c, 2 * (z | 1 << bit) + c) for c in range(2)] for z in lows]


def pack_kernel(me, upstream, factors, out, wide, mix, turned, in_sems, mix_sem, out_sems):
    place = Place(me)
    blocks = turned.shape[0]
    chunk = turned.shape[1] - BLOCK
    tiles = wide.shape[1] // ROWS
    count = in_sems.shape[0]
    edges = [ROWS * (tiles * i // count) for i in range(count + 1)]
    loads = [
        pltpu.make_async_copy(upstream.at[:, lo:hi], wide.at[:, lo:hi], in_sems.at[i])
        for i, (lo, hi) in enumerate(zip(edges, edges[1:]))
    ]
    load_mix = pltpu.make_async_copy(factors, mix, mix_sem)
    load_mix.start()
    for load in loads:
        load.start()
    load_mix.wait()
    row = place.first_row + iota((BLOCK, ROWS), 1)
    sides = []
    for side in range(2):
        level = jnp.minimum(2 * place.y + side, TOP)
        pick = lax.shift_right_logical(row, level + 5) % 2 * HALF + row % HALF
        sides.append((iota((BLOCK, ROWS), 0) == pick).astype(F32) + mix[level])
    tile = jnp.concatenate(sides, axis=0).T.astype(BF)
    for block in range(blocks):
        half = block % 2 * BLOCK
        turned[block, chunk:] = tile[half : half + BLOCK]
    stores = []
    group = blocks // out_sems.shape[0]
    for t in range(tiles):
        if t * ROWS in edges:
            loads[edges.index(t * ROWS)].wait()
        columns = wide[:, t * ROWS : (t + 1) * ROWS].T
        start, end = t * ROWS, (t + 1) * ROWS
        while start < end:
            block, at = start // chunk, start % chunk
            size = min(end - start, chunk - at)
            turned[block, at : at + size] = columns[start - t * ROWS : start - t * ROWS + size]
            start += size
        while len(stores) < out_sems.shape[0] and end >= (len(stores) + 1) * group * chunk:
            at = slice(len(stores) * group, (len(stores) + 1) * group)
            stores.append(pltpu.make_async_copy(turned.at[at], out.at[at], out_sems.at[len(stores)]))
            stores[-1].start()
    for store in stores:
        store.wait()


def pack(me, upstream, factors):
    rows, wide = upstream.shape
    shape = (2 * NZ, wide // (2 * NZ) + BLOCK, rows)
    hbm = pl.BlockSpec(memory_space=pltpu.HBM)
    return pl.pallas_call(
        pack_kernel,
        in_specs=[SCALARS, hbm, hbm],
        out_specs=hbm,
        out_shape=jax.ShapeDtypeStruct(shape, BF),
        scratch_shapes=[
            pltpu.VMEM((rows, wide), BF),
            pltpu.VMEM(factors.shape, F32),
            pltpu.VMEM(shape, BF),
            pltpu.SemaphoreType.DMA((4,)),
            pltpu.SemaphoreType.DMA,
            pltpu.SemaphoreType.DMA((4,)),
        ],
        compiler_params=pltpu.CompilerParams(vmem_limit_bytes=58 * 2**20),
        name="pack",
    )(me, upstream, factors)


def stack_kernel(me, *refs):
    *parts, _, out, top = refs
    place = Place(me)
    for k, part in enumerate(parts):
        out[k] = part[...]
    which = jnp.bitwise_xor(place.y, NY - 1)
    src, col = iota((ROWS, ROWS), 0), iota((ROWS, ROWS), 1)
    picks = []
    for j in range(4):
        pick = (col // HALF == j) & (src == HALF * (1 - place.x0) + col % HALF)
        picks.append(pick.astype(F32).astype(BF))
    for k in range(top.shape[0]):
        packed = dot(out[which, 4 * k], picks[0])
        for j in range(1, 4):
            packed = packed + dot(out[which, 4 * k + j], picks[j])
        top[k] = packed.astype(BF)


def stack(me, parts, after):
    blocks, rows, wide = parts[0].shape
    return pl.pallas_call(
        stack_kernel,
        in_specs=[SCALARS] + [WHOLE] * NY + [pl.BlockSpec(memory_space=pl.ANY)],
        out_specs=[WHOLE] * 2,
        out_shape=[
            jax.ShapeDtypeStruct((NY, blocks, rows, wide), BF),
            jax.ShapeDtypeStruct((blocks // 4, rows, wide), BF),
        ],
        compiler_params=PARAMS,
        name="stack",
    )(me, *parts, after)


def spreader(level, my_x):
    width = 2 * ROWS if 2 <= level < TOP else ROWS
    src, col = iota((ROWS, width), 0), iota((ROWS, width), 1)
    lane = level % 2 * BLOCK
    parts = 2 if level == 1 else 4
    keep = (src // HALF) % parts == (col // HALF) % parts
    if level == 0:
        picks, keep = [src == lane + col % BLOCK], src // BLOCK == col // BLOCK
    elif level == 1:
        picks = [src == lane + col // BLOCK * HALF + col % HALF]
    elif level < TOP:
        picks = [src == lane + col // ROWS * HALF + col % HALF]
    else:
        picks = [src == HALF * my_x + col % HALF] + [src == HALF * j + col % HALF for j in range(4)]
    return [pick.astype(F32).astype(BF) for pick in picks], keep


def expand_kernel(me, near, away, partner_near, partner_away, _, *refs):
    dense, held, sems = refs[:LEVELS], refs[LEVELS:-1], refs[-1]
    place = Place(me)
    first_core = place.core == 0
    loads = [[] for _ in range(NY)]
    for j in reversed(range(NY)):
        for c, ref in enumerate((near, away)):
            loads[j].append(pltpu.make_async_copy(ref.at[jnp.bitwise_xor(place.y, j)], held[c].at[j], sems.at[j, c]))
        if j == NY - 1:
            for c, ref in enumerate((partner_near, partner_away)):
                loads[j].append(pltpu.make_async_copy(ref, held[2 + c], sems.at[NY, c]))
        for load in loads[j]:
            load.start()

    def rows(one, other):
        return jnp.concatenate([jnp.where(first_core, one, other), jnp.where(first_core, other, one)], axis=0)

    for level in reversed(range(LEVELS)):
        if level == TOP or level % 2:
            for load in loads[level // 2]:
                load.wait()
        picks, keep = spreader(level, place.x0)
        for block in range(2 * NZ):
            full = dot(rows(held[0][level // 2, block], held[1][level // 2, block]), picks[0])
            dense[level][block, :, : full.shape[1]] = jnp.where(keep, full, 0.0).astype(BF)
            if level == TOP:
                far = dot(rows(held[2][block // 4], held[3][block // 4]), picks[1 + block % 4])
                dense[level][block, :, ROWS:] = jnp.where(keep, far, 0.0).astype(BF)


def expand(me, near, away, partner_near, partner_away, after):
    narrow, wide = (2 * NZ, ROWS, ROWS), (2 * NZ, ROWS, 2 * ROWS)
    return pl.pallas_call(
        expand_kernel,
        in_specs=[SCALARS] + [pl.BlockSpec(memory_space=pl.ANY)] * 5,
        out_specs=[WHOLE] * LEVELS,
        out_shape=[jax.ShapeDtypeStruct(narrow if level < 2 else wide, BF) for level in range(LEVELS)],
        scratch_shapes=[pltpu.VMEM(near.shape, BF)] * 2
        + [pltpu.VMEM(partner_near.shape, BF)] * 2
        + [pltpu.SemaphoreType.DMA((NY + 1, 2))],
        compiler_params=PARAMS,
        name="expand",
    )(me, near, away, partner_near, partner_away, after)


def grad_kernel(*refs):
    dense, mine, theirs, grads = refs[:TOP], refs[TOP], refs[TOP + 1], refs[TOP + 2 :]
    for level in range(TOP, 0, -1):
        mix, above, out_ref = dense[level - 1], grads[level] if level < TOP else None, grads[level - 1]
        for unit in units(level):
            for lo, hi in unit:
                if level == TOP:
                    both = jnp.concatenate([mine[lo], theirs[lo]], axis=1)
                    full = jnp.concatenate([mix[lo, :, :ROWS], mix[lo, :, ROWS:]], axis=0)
                elif level == 1:
                    both, full = above[lo], mix[lo]
                else:
                    both = jnp.concatenate([above[lo], above[hi]], axis=1)
                    full = jnp.concatenate([mix[lo], mix[hi]], axis=0)
                out = dot(both, full).astype(BF)
                out_ref[lo] = out[:, :ROWS]
                if hi is not None:
                    out_ref[hi] = out[:, ROWS:]


def grad_chain(dense, mine, theirs):
    return pl.pallas_call(
        grad_kernel,
        in_specs=[WHOLE] * (TOP + 2),
        out_specs=[WHOLE] * TOP,
        out_shape=[jax.ShapeDtypeStruct(mine.shape, BF)] * TOP,
        compiler_params=PARAMS,
        name="grad_chain",
    )(*dense, mine, theirs)


def fold(quad):
    lane = iota((HALF, ROWS), 1) // HALF
    out = quad[:HALF]
    for q in range(1, 4):
        out = jnp.where(lane == q, quad[q * HALF : (q + 1) * HALF], out)
    return out


def products(level, core, x_ref, grads, mine, theirs, out):
    def store(z, halves):
        for y in range(NY):
            piece = halves[y // 2][y % 2 * SLICE : (y % 2 + 1) * SLICE]
            out[y, z, level] = piece.astype(BF)

    if level < 3 or level == TOP:
        for z in range(NZ):
            block = 2 * z + core
            if level == TOP:
                quad = dot(x_ref[block], jnp.concatenate([mine[block], theirs[block]], axis=1))
                store(z, (fold(quad[:, :ROWS]), fold(quad[:, ROWS:])))
            elif level == 2:
                quad = dot(jnp.concatenate([x_ref[2 * z], x_ref[2 * z + 1]], axis=0), grads[level][block])
                store(z, (fold(quad[:ROWS]), fold(quad[ROWS:])))
            elif level == 1:
                quad = dot(x_ref[block], grads[level][block])
                even = (iota((HALF, ROWS), 1) // HALF) % 2 == 0
                rows = [quad[q * HALF : (q + 1) * HALF] for q in range(4)]
                store(z, (jnp.where(even, rows[0], rows[1]), jnp.where(even, rows[2], rows[3])))
            else:
                quad = dot(x_ref[block], grads[level][block])
                both = jnp.where(iota((BLOCK, ROWS), 1) < BLOCK, quad[:BLOCK], quad[BLOCK:])
                store(z, (both[:HALF], both[HALF:]))
        return
    bit = level - 3
    for lo in [z for z in range(NZ) if not z >> bit & 1]:
        hi = lo | 1 << bit
        x = jnp.concatenate([x_ref[2 * lo + core], x_ref[2 * hi + core]], axis=0)
        g = jnp.concatenate([grads[level][2 * lo + core], grads[level][2 * hi + core]], axis=1)
        quad = dot(x, g)
        for z, at in ((lo, slice(0, ROWS)), (hi, slice(ROWS, 2 * ROWS))):
            store(z, (fold(quad[:ROWS, at]), fold(quad[ROWS:, at])))


def forward_kernel(me, base, *refs):
    dense, grads = refs[:TOP], refs[TOP : 2 * TOP]
    mine, theirs, out, *states = refs[2 * TOP :]
    other = 1 - Place(me).core
    for block in range(2 * NZ):
        states[0][block] = base[block].T
    for level in range(LEVELS):
        if level < TOP:
            for lo, hi in [pair for unit in units(level) for pair in unit]:
                if hi is None:
                    states[level + 1][lo] = dot(dense[level][lo], states[level][lo]).astype(BF)
                else:
                    x = jnp.concatenate([states[level][lo], states[level][hi]], axis=0)
                    both = dot(jnp.concatenate([dense[level][lo], dense[level][hi]], axis=0), x).astype(BF)
                    states[level + 1][lo], states[level + 1][hi] = both[:ROWS], both[ROWS:]
        products(level, other, states[level], grads, mine, theirs, out)


def own_kernel(me, *refs):
    states, grads = refs[:LEVELS], refs[LEVELS : LEVELS + TOP]
    mine, theirs, out = refs[LEVELS + TOP :]
    for level in range(LEVELS):
        products(level, Place(me).core, states[level], grads, mine, theirs, out)


def forward(me, base, dense, grads, mine, theirs):
    blocks, wide, rows = base.shape
    shape = jax.ShapeDtypeStruct((NY, NZ, LEVELS, SLICE, rows), BF)
    out, *states = pl.pallas_call(
        forward_kernel,
        in_specs=[SCALARS] + [WHOLE] * (2 * TOP + 3),
        out_specs=[WHOLE] * (1 + LEVELS),
        out_shape=[shape] + [jax.ShapeDtypeStruct((blocks, rows, wide), BF)] * LEVELS,
        compiler_params=PARAMS,
        name="forward",
    )(me, base, *dense, *grads, mine, theirs)
    return out, states


def own_products(me, states, grads, mine, theirs):
    rows = mine.shape[2]
    return pl.pallas_call(
        own_kernel,
        in_specs=[SCALARS] + [WHOLE] * (LEVELS + TOP + 2),
        out_specs=WHOLE,
        out_shape=jax.ShapeDtypeStruct((NY, NZ, LEVELS, SLICE, rows), BF),
        compiler_params=PARAMS,
        name="own_products",
    )(me, *states, *grads, mine, theirs)


def call(kernel, shape, *args):
    return pl.pallas_call(
        kernel,
        in_specs=[SCALARS] + [WHOLE] * (len(args) - 1),
        out_specs=WHOLE,
        out_shape=shape,
        compiler_params=PARAMS,
        name=kernel.__name__,
    )(*args)


def core_sum(me, own, got, out):
    for y in range(NY):
        out[y] = (own[y].astype(F32) + got[y].astype(F32)).astype(BF)


def copies_of_sum(me, parts, out):
    total = parts[0].astype(F32)
    for k in range(1, parts.shape[0]):
        total = total + parts[k].astype(F32)
    for k in range(out.shape[0]):
        out[k] = total.astype(out.dtype)


def finish(me, slices, out):
    my_x = Place(me).x0
    own, other = my_x * NY, (1 - my_x) * NY
    for y in range(NY):
        at = slice(y * SLICE, (y + 1) * SLICE)
        out[:TOP, at] = slices[own + y, :TOP].astype(F32)
    near = [slices[own + y, TOP].astype(F32) for y in range(NY // 2)]
    far = [slices[other + y, TOP].astype(F32) for y in range(NY // 2, NY)]
    for h, (even, odd) in enumerate(((near, far), (far, near))):
        for y in range(NY // 2):
            at = h * HALF + y * SLICE
            out[TOP, at : at + SLICE] = jnp.where(my_x == 0, even[y], odd[y])


def per_device(codes, scales, factors, upstream):
    rows, wide = codes.shape
    blocks = 2 * NZ
    chunk = wide // blocks
    me = lax.axis_index(NAMES).astype(jnp.int32).reshape(1)

    got = lax.all_to_all(pack(me, upstream, factors.transpose(0, 2, 1)), ("z", "core"), 0, 0)
    mine, mixing = got[:, :chunk], got[:, chunk:]
    base = codes.astype(F32).reshape(rows, wide // rows, rows) * scales[0][None, :, None]
    base = base.reshape(rows, wide).astype(BF).T.reshape(blocks, chunk, rows)
    base = lax.all_to_all(base, ("z", "core"), 0, 0)
    theirs = lax.ppermute(mine, "x0", flips(2))

    near = [mixing] + [lax.ppermute(mixing, "y", flips(NY, k)) for k in range(1, NY)]
    near, top = stack(me, near, theirs)
    away = lax.ppermute(near, "core", flips(2))
    partner_near = lax.ppermute(top, "x0", flips(2))
    partner_away = lax.ppermute(top, ("x0", "core"), flips(4, 3))
    dense = expand(me, near, away, partner_near, partner_away, base)
    grads = grad_chain(dense[1:], mine, theirs)
    away, states = forward(me, base, dense[:TOP], grads, mine, theirs)
    got = lax.ppermute(away, "core", flips(2))
    own = own_products(me, states, grads, mine, theirs)

    part = (LEVELS, SLICE, rows)
    total = call(core_sum, jax.ShapeDtypeStruct(own.shape, BF), me, own, got)
    total = lax.all_to_all(total, "y", 0, 0)
    total = call(copies_of_sum, jax.ShapeDtypeStruct((2, NZ) + part, BF), me, total)
    total = lax.all_to_all(total.reshape((2 * NZ,) + part), ("zh", "z"), 0, 0)
    total = call(copies_of_sum, jax.ShapeDtypeStruct((2 * NY,) + part, BF), me, total)
    total = lax.all_to_all(total, ("x0", "y"), 0, 0)
    total = call(finish, jax.ShapeDtypeStruct((LEVELS, BLOCK, rows), F32), me, total)
    return total.transpose(0, 2, 1)


def solution(mesh):
    fsdp, col = mesh.devices.shape
    fine = Mesh(mesh.devices.reshape(fsdp // (4 * NZ), 2, NZ, 2, col // NY, NY), NAMES)
    rows, cols = ("x1", "x0", "z", "core"), ("zh", "y")
    return jax.shard_map(
        per_device,
        mesh=fine,
        in_specs=(P(rows, cols), P(rows, cols), P(None, rows, None), P(rows, cols)),
        out_specs=P(None, rows, None),
        check_vma=False,
    )
```

```python
import functools

import jax
import jax.numpy as jnp
from jax import lax
from jax.experimental import pallas as pl
from jax.experimental.pallas import tpu as pltpu
from jax.sharding import Mesh
from jax.sharding import PartitionSpec as P

BF = jnp.bfloat16
F32 = jnp.float32
HALF = 32
BLOCK = 2 * HALF
ROWS = 128
LEVELS = 7
TOP = LEVELS - 1
NZ = 8
NY = 4
SLICE = BLOCK // NY
NAMES = ("x1", "x0", "z", "core", "zh", "y")
PARAMS = pltpu.CompilerParams(vmem_limit_bytes=16 * 2**20)
WHOLE = pl.BlockSpec(memory_space=pltpu.VMEM)
SCALARS = pl.BlockSpec(memory_space=pltpu.SMEM)


class Place:
    def __init__(self, me):
        index = me[0]
        self.y, self.core, self.z, self.x0 = index & 3, index >> 3 & 1, index >> 4 & 7, index >> 7 & 1
        self.first_row = (index >> 3) * ROWS


def dot(a, b):
    return lax.dot_general(a, b, (((1,), (0,)), ((), ())), preferred_element_type=F32)


def iota(shape, dim):
    return lax.broadcasted_iota(jnp.int32, shape, dim)


def flips(count, distance=1):
    return [(i, i ^ distance) for i in range(count)]


def units(level):
    if level == 2:
        return [[(2 * z, 2 * z + 1)] for z in range(NZ)]
    if level < 2 or level == TOP:
        return [[(2 * z, None), (2 * z + 1, None)] for z in range(NZ)]
    bit = level - 3
    lows = [z for z in range(NZ) if not z >> bit & 1]
    return [[(2 * z + c, 2 * (z | 1 << bit) + c) for c in range(2)] for z in lows]


def pack_kernel(me, upstream, factors, out, wide, mix, turned, in_sems, mix_sems, out_sems):
    place = Place(me)
    blocks = turned.shape[0]
    chunk = turned.shape[1] - BLOCK
    tiles = wide.shape[1] // ROWS
    count = in_sems.shape[0]
    edges = [ROWS * (tiles * i // count) for i in range(count + 1)]
    loads = [
        pltpu.make_async_copy(upstream.at[:, lo:hi], wide.at[:, lo:hi], in_sems.at[i])
        for i, (lo, hi) in enumerate(zip(edges, edges[1:]))
    ]
    levels = [jnp.minimum(2 * place.y + side, TOP) for side in range(2)]
    load_mix = [pltpu.make_async_copy(factors.at[level], mix.at[i], mix_sems.at[i]) for i, level in enumerate(levels)]
    for load in load_mix + loads:
        load.start()
    for load in load_mix:
        load.wait()
    row = place.first_row + iota((BLOCK, ROWS), 1)
    sides = []
    for side, level in enumerate(levels):
        pick = lax.shift_right_logical(row, level + 5) % 2 * HALF + row % HALF
        sides.append((iota((BLOCK, ROWS), 0) == pick).astype(F32) + mix[side])
    tile = jnp.concatenate(sides, axis=0).T.astype(BF)
    for block in range(blocks):
        half = block % 2 * BLOCK
        turned[block, chunk:] = tile[half : half + BLOCK]
    stores = []
    group = blocks // out_sems.shape[0]
    for t in range(tiles):
        if t * ROWS in edges:
            loads[edges.index(t * ROWS)].wait()
        columns = wide[:, t * ROWS : (t + 1) * ROWS].T
        start, end = t * ROWS, (t + 1) * ROWS
        while start < end:
            block, at = start // chunk, start % chunk
            size = min(end - start, chunk - at)
            turned[block, at : at + size] = columns[start - t * ROWS : start - t * ROWS + size]
            start += size
        while len(stores) < out_sems.shape[0] and end >= (len(stores) + 1) * group * chunk:
            at = slice(len(stores) * group, (len(stores) + 1) * group)
            stores.append(pltpu.make_async_copy(turned.at[at], out.at[at], out_sems.at[len(stores)]))
            stores[-1].start()
    for store in stores:
        store.wait()


def pack(me, upstream, factors):
    rows, wide = upstream.shape
    shape = (2 * NZ, wide // (2 * NZ) + BLOCK, rows)
    hbm = pl.BlockSpec(memory_space=pltpu.HBM)
    return pl.pallas_call(
        pack_kernel,
        in_specs=[SCALARS, hbm, hbm],
        out_specs=hbm,
        out_shape=jax.ShapeDtypeStruct(shape, BF),
        scratch_shapes=[
            pltpu.VMEM((rows, wide), BF),
            pltpu.VMEM((2,) + factors.shape[1:], F32),
            pltpu.VMEM(shape, BF),
            pltpu.SemaphoreType.DMA((4,)),
            pltpu.SemaphoreType.DMA((2,)),
            pltpu.SemaphoreType.DMA((4,)),
        ],
        compiler_params=pltpu.CompilerParams(vmem_limit_bytes=58 * 2**20),
        name="pack",
    )(me, upstream, factors)


def stack_kernel(me, *refs):
    *parts, _, out, top = refs
    place = Place(me)
    for k, part in enumerate(parts):
        out[k] = part[...]
    which = jnp.bitwise_xor(place.y, NY - 1)
    src, col = iota((ROWS, ROWS), 0), iota((ROWS, ROWS), 1)
    picks = []
    for j in range(4):
        pick = (col // HALF == j) & (src == HALF * (1 - place.x0) + col % HALF)
        picks.append(pick.astype(F32).astype(BF))
    for k in range(top.shape[0]):
        packed = dot(out[which, 4 * k], picks[0])
        for j in range(1, 4):
            packed = packed + dot(out[which, 4 * k + j], picks[j])
        top[k] = packed.astype(BF)


def stack(me, parts, after):
    blocks, rows, wide = parts[0].shape
    return pl.pallas_call(
        stack_kernel,
        in_specs=[SCALARS] + [WHOLE] * NY + [pl.BlockSpec(memory_space=pl.ANY)],
        out_specs=[WHOLE] * 2,
        out_shape=[
            jax.ShapeDtypeStruct((NY, blocks, rows, wide), BF),
            jax.ShapeDtypeStruct((blocks // 4, rows, wide), BF),
        ],
        compiler_params=PARAMS,
        name="stack",
    )(me, *parts, after)


def spreader(level, my_x):
    width = 2 * ROWS if 2 <= level < TOP else ROWS
    src, col = iota((ROWS, width), 0), iota((ROWS, width), 1)
    lane = level % 2 * BLOCK
    parts = 2 if level == 1 else 4
    keep = (src // HALF) % parts == (col // HALF) % parts
    if level == 0:
        picks, keep = [src == lane + col % BLOCK], src // BLOCK == col // BLOCK
    elif level == 1:
        picks = [src == lane + col // BLOCK * HALF + col % HALF]
    elif level < TOP:
        picks = [src == lane + col // ROWS * HALF + col % HALF]
    else:
        picks = [src == HALF * my_x + col % HALF] + [src == HALF * j + col % HALF for j in range(4)]
    return [pick.astype(F32).astype(BF) for pick in picks], keep


def expand_kernel(me, near, away, partner_near, partner_away, _, *refs):
    dense, held, sems = refs[:LEVELS], refs[LEVELS:-1], refs[-1]
    place = Place(me)
    first_core = place.core == 0
    loads = [[] for _ in range(NY)]
    for j in reversed(range(NY)):
        for c, ref in enumerate((near, away)):
            loads[j].append(pltpu.make_async_copy(ref.at[jnp.bitwise_xor(place.y, j)], held[c].at[j], sems.at[j, c]))
        if j == NY - 1:
            for c, ref in enumerate((partner_near, partner_away)):
                loads[j].append(pltpu.make_async_copy(ref, held[2 + c], sems.at[NY, c]))
        for load in loads[j]:
            load.start()

    def rows(one, other):
        return jnp.concatenate([jnp.where(first_core, one, other), jnp.where(first_core, other, one)], axis=0)

    for level in reversed(range(LEVELS)):
        if level == TOP or level % 2:
            for load in loads[level // 2]:
                load.wait()
        picks, keep = spreader(level, place.x0)
        for block in range(2 * NZ):
            full = dot(rows(held[0][level // 2, block], held[1][level // 2, block]), picks[0])
            dense[level][block, :, : full.shape[1]] = jnp.where(keep, full, 0.0).astype(BF)
            if level == TOP:
                far = dot(rows(held[2][block // 4], held[3][block // 4]), picks[1 + block % 4])
                dense[level][block, :, ROWS:] = jnp.where(keep, far, 0.0).astype(BF)


def expand(me, near, away, partner_near, partner_away, after):
    narrow, wide = (2 * NZ, ROWS, ROWS), (2 * NZ, ROWS, 2 * ROWS)
    return pl.pallas_call(
        expand_kernel,
        in_specs=[SCALARS] + [pl.BlockSpec(memory_space=pl.ANY)] * 5,
        out_specs=[WHOLE] * LEVELS,
        out_shape=[jax.ShapeDtypeStruct(narrow if level < 2 else wide, BF) for level in range(LEVELS)],
        scratch_shapes=[pltpu.VMEM(near.shape, BF)] * 2
        + [pltpu.VMEM(partner_near.shape, BF)] * 2
        + [pltpu.SemaphoreType.DMA((NY + 1, 2))],
        compiler_params=PARAMS,
        name="expand",
    )(me, near, away, partner_near, partner_away, after)


def grad_step(level, mix, above, mine, theirs, below):
    for lo, hi in [pair for unit in units(level) for pair in unit]:
        if level == TOP:
            both = jnp.concatenate([mine[lo], theirs[lo]], axis=1)
            full = jnp.concatenate([mix[lo, :, :ROWS], mix[lo, :, ROWS:]], axis=0)
        elif level == 1:
            both, full = above[lo], mix[lo]
        else:
            both = jnp.concatenate([above[lo], above[hi]], axis=1)
            full = jnp.concatenate([mix[lo], mix[hi]], axis=0)
        out = dot(both, full).astype(BF)
        below[lo] = out[:, :ROWS]
        if hi is not None:
            below[hi] = out[:, ROWS:]


def forward_step(level, mix, x_ref, after):
    for lo, hi in [pair for unit in units(level) for pair in unit]:
        if hi is None:
            after[lo] = dot(mix[lo], x_ref[lo]).astype(BF)
        else:
            x = jnp.concatenate([x_ref[lo], x_ref[hi]], axis=0)
            both = dot(jnp.concatenate([mix[lo], mix[hi]], axis=0), x).astype(BF)
            after[lo], after[hi] = both[:ROWS], both[ROWS:]


def fold(quad):
    lane = iota((HALF, ROWS), 1) // HALF
    out = quad[:HALF]
    for q in range(1, 4):
        out = jnp.where(lane == q, quad[q * HALF : (q + 1) * HALF], out)
    return out


def products(level, core, x_ref, grads, mine, theirs, out):
    def store(z, halves):
        for y in range(NY):
            piece = halves[y // 2][y % 2 * SLICE : (y % 2 + 1) * SLICE]
            out[y, z, level] = piece.astype(BF)

    if level < 3 or level == TOP:
        for z in range(NZ):
            block = 2 * z + core
            if level == TOP:
                quad = dot(x_ref[block], jnp.concatenate([mine[block], theirs[block]], axis=1))
                store(z, (fold(quad[:, :ROWS]), fold(quad[:, ROWS:])))
            elif level == 2:
                quad = dot(jnp.concatenate([x_ref[2 * z], x_ref[2 * z + 1]], axis=0), grads[level][block])
                store(z, (fold(quad[:ROWS]), fold(quad[ROWS:])))
            elif level == 1:
                quad = dot(x_ref[block], grads[level][block])
                even = (iota((HALF, ROWS), 1) // HALF) % 2 == 0
                rows = [quad[q * HALF : (q + 1) * HALF] for q in range(4)]
                store(z, (jnp.where(even, rows[0], rows[1]), jnp.where(even, rows[2], rows[3])))
            else:
                quad = dot(x_ref[block], grads[level][block])
                both = jnp.where(iota((BLOCK, ROWS), 1) < BLOCK, quad[:BLOCK], quad[BLOCK:])
                store(z, (both[:HALF], both[HALF:]))
        return
    bit = level - 3
    for lo in [z for z in range(NZ) if not z >> bit & 1]:
        hi = lo | 1 << bit
        x = jnp.concatenate([x_ref[2 * lo + core], x_ref[2 * hi + core]], axis=0)
        g = jnp.concatenate([grads[level][2 * lo + core], grads[level][2 * hi + core]], axis=1)
        quad = dot(x, g)
        for z, at in ((lo, slice(0, ROWS)), (hi, slice(ROWS, 2 * ROWS))):
            store(z, (fold(quad[:ROWS, at]), fold(quad[ROWS:, at])))


def chain_kernel(me, base, *refs):
    dense, (mine, theirs, out) = refs[:LEVELS], refs[LEVELS : LEVELS + 3]
    grads, states = refs[LEVELS + 3 : LEVELS + 3 + TOP], refs[LEVELS + 3 + TOP :]
    other = 1 - Place(me).core
    for block in range(2 * NZ):
        states[0][block] = base[block].T
    for step in range(TOP):
        level = TOP - step
        grad_step(level, dense[level], grads[level] if level < TOP else None, mine, theirs, grads[level - 1])
        forward_step(step, dense[step], states[step], states[step + 1])
    for level in range(LEVELS):
        products(level, other, states[level], grads, mine, theirs, out)


def own_kernel(me, *refs):
    states, grads = refs[:LEVELS], refs[LEVELS : LEVELS + TOP]
    mine, theirs, out = refs[LEVELS + TOP :]
    for level in range(LEVELS):
        products(level, Place(me).core, states[level], grads, mine, theirs, out)


def chains(me, base, dense, mine, theirs):
    blocks, wide, rows = base.shape
    results = pl.pallas_call(
        chain_kernel,
        in_specs=[SCALARS] + [WHOLE] * (LEVELS + 3),
        out_specs=[WHOLE] * (1 + TOP + LEVELS),
        out_shape=[jax.ShapeDtypeStruct((NY, NZ, LEVELS, SLICE, rows), BF)]
        + [jax.ShapeDtypeStruct(base.shape, BF)] * TOP
        + [jax.ShapeDtypeStruct((blocks, rows, wide), BF)] * LEVELS,
        compiler_params=PARAMS,
        name="chains",
    )(me, base, *dense, mine, theirs)
    return results[0], results[1 : 1 + TOP], results[1 + TOP :]


def own_products(me, states, grads, mine, theirs):
    rows = mine.shape[2]
    return pl.pallas_call(
        own_kernel,
        in_specs=[SCALARS] + [WHOLE] * (LEVELS + TOP + 2),
        out_specs=WHOLE,
        out_shape=jax.ShapeDtypeStruct((NY, NZ, LEVELS, SLICE, rows), BF),
        compiler_params=PARAMS,
        name="own_products",
    )(me, *states, *grads, mine, theirs)


def call(kernel, shape, *args):
    return pl.pallas_call(
        kernel,
        in_specs=[SCALARS] + [WHOLE] * (len(args) - 1),
        out_specs=WHOLE,
        out_shape=shape,
        compiler_params=PARAMS,
        name=kernel.__name__,
    )(*args)


def core_sum(me, own, got, out):
    for y in range(NY):
        out[y] = (own[y].astype(F32) + got[y].astype(F32)).astype(BF)


def copies_of_sum(me, parts, out):
    total = parts[0].astype(F32)
    for k in range(1, parts.shape[0]):
        total = total + parts[k].astype(F32)
    for k in range(out.shape[0]):
        out[k] = total.astype(out.dtype)


def finish(me, slices, out):
    my_x = Place(me).x0
    own, other = my_x * NY, (1 - my_x) * NY
    for y in range(NY):
        at = slice(y * SLICE, (y + 1) * SLICE)
        out[:TOP, at] = slices[own + y, :TOP].astype(F32)
    near = [slices[own + y, TOP].astype(F32) for y in range(NY // 2)]
    far = [slices[other + y, TOP].astype(F32) for y in range(NY // 2, NY)]
    for h, (even, odd) in enumerate(((near, far), (far, near))):
        for y in range(NY // 2):
            at = h * HALF + y * SLICE
            out[TOP, at : at + SLICE] = jnp.where(my_x == 0, even[y], odd[y])


def per_device(codes, scales, factors, upstream):
    rows, wide = codes.shape
    blocks = 2 * NZ
    chunk = wide // blocks
    me = lax.axis_index(NAMES).astype(jnp.int32).reshape(1)

    got = lax.all_to_all(pack(me, upstream, factors.transpose(0, 2, 1)), ("z", "core"), 0, 0)
    mine, mixing = got[:, :chunk], got[:, chunk:]
    base = codes.astype(F32).reshape(rows, wide // rows, rows) * scales[0][None, :, None]
    base = base.reshape(rows, wide).astype(BF).T.reshape(blocks, chunk, rows)
    base = lax.all_to_all(base, ("z", "core"), 0, 0)
    theirs = lax.ppermute(mine, "x0", flips(2))

    near = [mixing] + [lax.ppermute(mixing, "y", flips(NY, k)) for k in range(1, NY)]
    near, top = stack(me, near, theirs)
    away = lax.ppermute(near, "core", flips(2))
    partner_near = lax.ppermute(top, "x0", flips(2))
    partner_away = lax.ppermute(top, ("x0", "core"), flips(4, 3))
    dense = expand(me, near, away, partner_near, partner_away, base)
    away, grads, states = chains(me, base, dense, mine, theirs)
    got = lax.ppermute(away, "core", flips(2))
    own = own_products(me, states, grads, mine, theirs)

    part = (LEVELS, SLICE, rows)
    total = call(core_sum, jax.ShapeDtypeStruct(own.shape, BF), me, own, got)
    total = lax.all_to_all(total, "y", 0, 0)
    total = call(copies_of_sum, jax.ShapeDtypeStruct((2, NZ) + part, BF), me, total)
    total = lax.all_to_all(total.reshape((2 * NZ,) + part), ("zh", "z"), 0, 0)
    total = call(copies_of_sum, jax.ShapeDtypeStruct((2 * NY,) + part, BF), me, total)
    total = lax.all_to_all(total, ("x0", "y"), 0, 0)
    total = call(finish, jax.ShapeDtypeStruct((LEVELS, BLOCK, rows), F32), me, total)
    return total.transpose(0, 2, 1)


def solution(mesh):
    fsdp, col = mesh.devices.shape
    fine = Mesh(mesh.devices.reshape(fsdp // (4 * NZ), 2, NZ, 2, col // NY, NY), NAMES)
    rows, cols = ("x1", "x0", "z", "core"), ("zh", "y")
    return jax.shard_map(
        per_device,
        mesh=fine,
        in_specs=(P(rows, cols), P(rows, cols), P(None, rows, None), P(rows, cols)),
        out_specs=P(None, rows, None),
        check_vma=False,
    )
```

```python
import functools

import jax
import jax.numpy as jnp
from jax import lax
from jax.experimental import pallas as pl
from jax.experimental.pallas import tpu as pltpu
from jax.sharding import Mesh
from jax.sharding import PartitionSpec as P

BF = jnp.bfloat16
F32 = jnp.float32
HALF = 32
BLOCK = 2 * HALF
ROWS = 128
LEVELS = 7
TOP = LEVELS - 1
NZ = 8
NY = 4
SLICE = BLOCK // NY
NAMES = ("x1", "x0", "z", "core", "zh", "y")
PARAMS = pltpu.CompilerParams(vmem_limit_bytes=16 * 2**20)
WHOLE = pl.BlockSpec(memory_space=pltpu.VMEM)
SCALARS = pl.BlockSpec(memory_space=pltpu.SMEM)


class Place:
    def __init__(self, me):
        index = me[0]
        self.y, self.core, self.z, self.x0 = index & 3, index >> 3 & 1, index >> 4 & 7, index >> 7 & 1
        self.first_row = (index >> 3) * ROWS


def dot(a, b):
    return lax.dot_general(a, b, (((1,), (0,)), ((), ())), preferred_element_type=F32)


def iota(shape, dim):
    return lax.broadcasted_iota(jnp.int32, shape, dim)


def flips(count, distance=1):
    return [(i, i ^ distance) for i in range(count)]


def units(level):
    if level == 2:
        return [[(2 * z, 2 * z + 1)] for z in range(NZ)]
    if level < 2 or level == TOP:
        return [[(2 * z, None), (2 * z + 1, None)] for z in range(NZ)]
    bit = level - 3
    lows = [z for z in range(NZ) if not z >> bit & 1]
    return [[(2 * z + c, 2 * (z | 1 << bit) + c) for c in range(2)] for z in lows]


def pack_kernel(me, upstream, factors, out, wide, mix, turned, in_sems, mix_sems, out_sems):
    place = Place(me)
    blocks = turned.shape[0]
    chunk = turned.shape[1] - BLOCK
    tiles = wide.shape[1] // ROWS
    count = in_sems.shape[0]
    edges = [ROWS * (tiles * i // count) for i in range(count + 1)]
    loads = [
        pltpu.make_async_copy(upstream.at[:, lo:hi], wide.at[:, lo:hi], in_sems.at[i])
        for i, (lo, hi) in enumerate(zip(edges, edges[1:]))
    ]
    levels = [jnp.minimum(2 * place.y + side, TOP) for side in range(2)]
    load_mix = [pltpu.make_async_copy(factors.at[level], mix.at[i], mix_sems.at[i]) for i, level in enumerate(levels)]
    for load in load_mix + loads:
        load.start()
    for load in load_mix:
        load.wait()
    row = place.first_row + iota((BLOCK, ROWS), 1)
    sides = []
    for side, level in enumerate(levels):
        pick = lax.shift_right_logical(row, level + 5) % 2 * HALF + row % HALF
        sides.append((iota((BLOCK, ROWS), 0) == pick).astype(F32) + mix[side])
    sides[1] = jnp.where(place.y == NY - 1, pltpu.roll(sides[1], BLOCK, 1), sides[1])
    tile = jnp.concatenate(sides, axis=0).T.astype(BF)
    for block in range(blocks):
        half = block % 2 * BLOCK
        turned[block, chunk:] = tile[half : half + BLOCK]
    stores = []
    group = blocks // out_sems.shape[0]
    for t in range(tiles):
        if t * ROWS in edges:
            loads[edges.index(t * ROWS)].wait()
        columns = wide[:, t * ROWS : (t + 1) * ROWS].T
        start, end = t * ROWS, (t + 1) * ROWS
        while start < end:
            block, at = start // chunk, start % chunk
            size = min(end - start, chunk - at)
            turned[block, at : at + size] = columns[start - t * ROWS : start - t * ROWS + size]
            start += size
        while len(stores) < out_sems.shape[0] and end >= (len(stores) + 1) * group * chunk:
            at = slice(len(stores) * group, (len(stores) + 1) * group)
            stores.append(pltpu.make_async_copy(turned.at[at], out.at[at], out_sems.at[len(stores)]))
            stores[-1].start()
    for store in stores:
        store.wait()


def pack(me, upstream, factors):
    rows, wide = upstream.shape
    shape = (2 * NZ, wide // (2 * NZ) + BLOCK, rows)
    hbm = pl.BlockSpec(memory_space=pltpu.HBM)
    return pl.pallas_call(
        pack_kernel,
        in_specs=[SCALARS, hbm, hbm],
        out_specs=hbm,
        out_shape=jax.ShapeDtypeStruct(shape, BF),
        scratch_shapes=[
            pltpu.VMEM((rows, wide), BF),
            pltpu.VMEM((2,) + factors.shape[1:], F32),
            pltpu.VMEM(shape, BF),
            pltpu.SemaphoreType.DMA((4,)),
            pltpu.SemaphoreType.DMA((2,)),
            pltpu.SemaphoreType.DMA((4,)),
        ],
        compiler_params=pltpu.CompilerParams(vmem_limit_bytes=58 * 2**20),
        name="pack",
    )(me, upstream, factors)


def stack_kernel(me, *refs):
    *parts, _, out, top = refs
    place = Place(me)
    for k, part in enumerate(parts):
        out[k] = part[...]
    which = jnp.bitwise_xor(place.y, NY - 1)
    src, col = iota((ROWS, ROWS), 0), iota((ROWS, ROWS), 1)
    for h in range(2):
        picks = []
        for j in range(4):
            pick = (col // HALF == j) & (src == h * BLOCK + HALF * (1 - place.x0) + col % HALF)
            picks.append(pick.astype(F32).astype(BF))
        count = top.shape[0] // 2
        for k in range(count):
            packed = dot(out[which, 4 * k], picks[0])
            for j in range(1, 4):
                packed = packed + dot(out[which, 4 * k + j], picks[j])
            top[h * count + k] = packed.astype(BF)


def stack(me, parts, after):
    blocks, rows, wide = parts[0].shape
    return pl.pallas_call(
        stack_kernel,
        in_specs=[SCALARS] + [WHOLE] * NY + [pl.BlockSpec(memory_space=pl.ANY)],
        out_specs=[WHOLE] * 2,
        out_shape=[
            jax.ShapeDtypeStruct((NY, blocks, rows, wide), BF),
            jax.ShapeDtypeStruct((blocks // 2, rows, wide), BF),
        ],
        compiler_params=PARAMS,
        name="stack",
    )(me, *parts, after)


def spreader(level, my_x):
    width = 2 * ROWS if 2 <= level < TOP else ROWS
    src, col = iota((ROWS, width), 0), iota((ROWS, width), 1)
    lane = level % 2 * BLOCK
    parts = 2 if level == 1 else 4
    keep = (src // HALF) % parts == (col // HALF) % parts
    if level == 0:
        picks, keep = [src == lane + col % BLOCK], src // BLOCK == col // BLOCK
    elif level == 1:
        picks = [src == lane + col // BLOCK * HALF + col % HALF]
    elif level < TOP:
        picks = [src == lane + col // ROWS * HALF + col % HALF]
    else:
        picks = [src == HALF * my_x + col % HALF] + [src == HALF * j + col % HALF for j in range(4)]
    return [pick.astype(F32).astype(BF) for pick in picks], keep


def top_kernel(me, near, halves, mine, theirs, out, held, sem):
    place = Place(me)
    first_core = place.core == 0
    load = pltpu.make_async_copy(near.at[jnp.bitwise_xor(place.y, NY - 1)], held, sem)
    load.start()
    load.wait()
    src, col = iota((ROWS, ROWS), 0), iota((ROWS, ROWS), 1)
    keep = src // HALF == col // HALF
    own = [(src == h * BLOCK + HALF * place.x0 + col % HALF).astype(F32).astype(BF) for h in range(2)]
    far = [(src == HALF * j + col % HALF).astype(F32).astype(BF) for j in range(4)]
    count = halves.shape[0] // 2

    def rows(one, other):
        low, high = jnp.where(first_core, one, other), jnp.where(first_core, other, one)
        return jnp.where(keep, jnp.concatenate([low, high], axis=0), 0.0).astype(BF)

    for block in range(2 * NZ):
        k, pick = block // 4, far[block % 4]
        full = [rows(dot(held[block], own[0]), dot(held[block], own[1]))]
        full.append(rows(dot(halves[k], pick), dot(halves[count + k], pick)))
        both = jnp.concatenate([mine[block], theirs[block]], axis=1)
        out[block] = dot(both, jnp.concatenate(full, axis=0)).astype(BF)


def top_grad(me, near, halves, mine, theirs):
    return pl.pallas_call(
        top_kernel,
        in_specs=[SCALARS, pl.BlockSpec(memory_space=pl.ANY)] + [WHOLE] * 3,
        out_specs=WHOLE,
        out_shape=jax.ShapeDtypeStruct(mine.shape, BF),
        scratch_shapes=[pltpu.VMEM(near.shape[1:], BF), pltpu.SemaphoreType.DMA],
        compiler_params=PARAMS,
        name="top_grad",
    )(me, near, halves, mine, theirs)


def spread(level, place, whole, dense):
    picks, keep = spreader(level, place.x0)
    for block in range(2 * NZ):
        full = dot(whole(block), picks[0])
        dense[block, :, : full.shape[1]] = jnp.where(keep, full, 0.0).astype(BF)


def dense_shape(level):
    return jax.ShapeDtypeStruct((2 * NZ, ROWS, ROWS if level < 2 else 2 * ROWS), BF)


def expand_kernel(me, near, away, _, *refs):
    dense, held, sems = refs[:TOP], refs[TOP:-1], refs[-1]
    place = Place(me)
    first_core = place.core == 0
    loads = [
        [
            pltpu.make_async_copy(ref.at[jnp.bitwise_xor(place.y, j)], held[c].at[j], sems.at[j, c])
            for c, ref in enumerate((near, away))
        ]
        for j in range(TOP // 2)
    ]
    for pair in loads:
        for load in pair:
            load.start()

    for level in range(TOP):
        j = level // 2
        if level % 2 == 0:
            for load in loads[j]:
                load.wait()

        def whole(block):
            one, other = held[0][j, block], held[1][j, block]
            return jnp.concatenate([jnp.where(first_core, one, other), jnp.where(first_core, other, one)], axis=0)

        spread(level, place, whole, dense[level])


def expand(me, near, away, after):
    held = pltpu.VMEM((TOP // 2,) + near.shape[1:], BF)
    return pl.pallas_call(
        expand_kernel,
        in_specs=[SCALARS] + [pl.BlockSpec(memory_space=pl.ANY)] * 3,
        out_specs=[WHOLE] * TOP,
        out_shape=[dense_shape(level) for level in range(TOP)],
        scratch_shapes=[held, held, pltpu.SemaphoreType.DMA((TOP // 2, 2))],
        compiler_params=PARAMS,
        name="expand",
    )(me, near, away, after)


def grad_step(level, mix, above, below):
    for lo, hi in [pair for unit in units(level) for pair in unit]:
        if level == 1:
            both, full = above[lo], mix[lo]
        else:
            both = jnp.concatenate([above[lo], above[hi]], axis=1)
            full = jnp.concatenate([mix[lo], mix[hi]], axis=0)
        out = dot(both, full).astype(BF)
        below[lo] = out[:, :ROWS]
        if hi is not None:
            below[hi] = out[:, ROWS:]


def forward_step(level, mix, x_ref, after):
    for lo, hi in [pair for unit in units(level) for pair in unit]:
        if hi is None:
            after[lo] = dot(mix[lo], x_ref[lo]).astype(BF)
        else:
            x = jnp.concatenate([x_ref[lo], x_ref[hi]], axis=0)
            both = dot(jnp.concatenate([mix[lo], mix[hi]], axis=0), x).astype(BF)
            after[lo], after[hi] = both[:ROWS], both[ROWS:]


def fold(quad):
    lane = iota((HALF, ROWS), 1) // HALF
    out = quad[:HALF]
    for q in range(1, 4):
        out = jnp.where(lane == q, quad[q * HALF : (q + 1) * HALF], out)
    return out


def products(level, core, x_ref, grads, mine, theirs, out):
    def store(z, halves):
        for y in range(NY):
            piece = halves[y // 2][y % 2 * SLICE : (y % 2 + 1) * SLICE]
            out[y, z, level] = piece.astype(BF)

    if level < 3 or level == TOP:
        for z in range(NZ):
            block = 2 * z + core
            if level == TOP:
                quad = dot(x_ref[block], jnp.concatenate([mine[block], theirs[block]], axis=1))
                store(z, (fold(quad[:, :ROWS]), fold(quad[:, ROWS:])))
            elif level == 2:
                quad = dot(jnp.concatenate([x_ref[2 * z], x_ref[2 * z + 1]], axis=0), grads[level][block])
                store(z, (fold(quad[:ROWS]), fold(quad[ROWS:])))
            elif level == 1:
                quad = dot(x_ref[block], grads[level][block])
                even = (iota((HALF, ROWS), 1) // HALF) % 2 == 0
                rows = [quad[q * HALF : (q + 1) * HALF] for q in range(4)]
                store(z, (jnp.where(even, rows[0], rows[1]), jnp.where(even, rows[2], rows[3])))
            else:
                quad = dot(x_ref[block], grads[level][block])
                both = jnp.where(iota((BLOCK, ROWS), 1) < BLOCK, quad[:BLOCK], quad[BLOCK:])
                store(z, (both[:HALF], both[HALF:]))
        return
    bit = level - 3
    for lo in [z for z in range(NZ) if not z >> bit & 1]:
        hi = lo | 1 << bit
        x = jnp.concatenate([x_ref[2 * lo + core], x_ref[2 * hi + core]], axis=0)
        g = jnp.concatenate([grads[level][2 * lo + core], grads[level][2 * hi + core]], axis=1)
        quad = dot(x, g)
        for z, at in ((lo, slice(0, ROWS)), (hi, slice(ROWS, 2 * ROWS))):
            store(z, (fold(quad[:ROWS, at]), fold(quad[ROWS:, at])))


def chain_kernel(me, base, *refs):
    dense, (top, mine, theirs, out) = refs[:TOP], refs[TOP : TOP + 4]
    grads, states = refs[TOP + 4 : 2 * TOP + 3] + (top,), refs[2 * TOP + 3 :]
    other = 1 - Place(me).core
    for block in range(2 * NZ):
        states[0][block] = base[block].T
    for step in range(TOP):
        level = TOP - 1 - step
        if level:
            grad_step(level, dense[level], grads[level], grads[level - 1])
        forward_step(step, dense[step], states[step], states[step + 1])
    for level in range(LEVELS):
        products(level, other, states[level], grads, mine, theirs, out)


def own_kernel(me, *refs):
    states, grads = refs[:LEVELS], refs[LEVELS : LEVELS + TOP]
    mine, theirs, out = refs[LEVELS + TOP :]
    for level in range(LEVELS):
        products(level, Place(me).core, states[level], grads, mine, theirs, out)


def chains(me, base, dense, top, mine, theirs):
    blocks, wide, rows = base.shape
    results = pl.pallas_call(
        chain_kernel,
        in_specs=[SCALARS] + [WHOLE] * (TOP + 4),
        out_specs=[WHOLE] * (TOP + LEVELS),
        out_shape=[jax.ShapeDtypeStruct((NY, NZ, LEVELS, SLICE, rows), BF)]
        + [jax.ShapeDtypeStruct(base.shape, BF)] * (TOP - 1)
        + [jax.ShapeDtypeStruct((blocks, rows, wide), BF)] * LEVELS,
        compiler_params=PARAMS,
        name="chains",
    )(me, base, *dense, top, mine, theirs)
    return results[0], [*results[1:TOP], top], results[TOP:]


def own_products(me, states, grads, mine, theirs):
    rows = mine.shape[2]
    return pl.pallas_call(
        own_kernel,
        in_specs=[SCALARS] + [WHOLE] * (LEVELS + TOP + 2),
        out_specs=WHOLE,
        out_shape=jax.ShapeDtypeStruct((NY, NZ, LEVELS, SLICE, rows), BF),
        compiler_params=PARAMS,
        name="own_products",
    )(me, *states, *grads, mine, theirs)


def call(kernel, shape, *args):
    return pl.pallas_call(
        kernel,
        in_specs=[SCALARS] + [WHOLE] * (len(args) - 1),
        out_specs=WHOLE,
        out_shape=shape,
        compiler_params=PARAMS,
        name=kernel.__name__,
    )(*args)


def core_sum(me, own, got, out):
    for y in range(NY):
        out[y] = (own[y].astype(F32) + got[y].astype(F32)).astype(BF)


def copies_of_sum(me, parts, out):
    total = parts[0].astype(F32)
    for k in range(1, parts.shape[0]):
        total = total + parts[k].astype(F32)
    for k in range(out.shape[0]):
        out[k] = total.astype(out.dtype)


def finish(me, slices, out):
    my_x = Place(me).x0
    own, other = my_x * NY, (1 - my_x) * NY
    for y in range(NY):
        at = slice(y * SLICE, (y + 1) * SLICE)
        out[:TOP, at] = slices[own + y, :TOP].astype(F32)
    near = [slices[own + y, TOP].astype(F32) for y in range(NY // 2)]
    far = [slices[other + y, TOP].astype(F32) for y in range(NY // 2, NY)]
    for h, (even, odd) in enumerate(((near, far), (far, near))):
        for y in range(NY // 2):
            at = h * HALF + y * SLICE
            out[TOP, at : at + SLICE] = jnp.where(my_x == 0, even[y], odd[y])


def per_device(codes, scales, factors, upstream):
    rows, wide = codes.shape
    blocks = 2 * NZ
    chunk = wide // blocks
    me = lax.axis_index(NAMES).astype(jnp.int32).reshape(1)

    got = lax.all_to_all(pack(me, upstream, factors.transpose(0, 2, 1)), ("z", "core"), 0, 0)
    mine, mixing = got[:, :chunk], got[:, chunk:]
    base = codes.astype(F32).reshape(rows, wide // rows, rows) * scales[0][None, :, None]
    base = base.reshape(rows, wide).astype(BF).T.reshape(blocks, chunk, rows)
    base = lax.all_to_all(base, ("z", "core"), 0, 0)
    theirs = lax.ppermute(mine, "x0", flips(2))

    near = [mixing] + [lax.ppermute(mixing, "y", flips(NY, k)) for k in range(1, NY)]
    near, top = stack(me, near, theirs)
    away = lax.ppermute(near, "core", flips(2))
    halves = lax.ppermute(top, "x0", flips(2))
    top = top_grad(me, near, halves, mine, theirs)
    dense = expand(me, near, away, base)
    away, grads, states = chains(me, base, dense, top, mine, theirs)
    got = lax.ppermute(away, "core", flips(2))
    own = own_products(me, states, grads, mine, theirs)

    part = (LEVELS, SLICE, rows)
    total = call(core_sum, jax.ShapeDtypeStruct(own.shape, BF), me, own, got)
    total = lax.all_to_all(total, "y", 0, 0)
    total = call(copies_of_sum, jax.ShapeDtypeStruct((2, NZ) + part, BF), me, total)
    total = lax.all_to_all(total.reshape((2 * NZ,) + part), ("zh", "z"), 0, 0)
    total = call(copies_of_sum, jax.ShapeDtypeStruct((2 * NY,) + part, BF), me, total)
    total = lax.all_to_all(total, ("x0", "y"), 0, 0)
    total = call(finish, jax.ShapeDtypeStruct((LEVELS, BLOCK, rows), F32), me, total)
    return total.transpose(0, 2, 1)


def solution(mesh):
    fsdp, col = mesh.devices.shape
    fine = Mesh(mesh.devices.reshape(fsdp // (4 * NZ), 2, NZ, 2, col // NY, NY), NAMES)
    rows, cols = ("x1", "x0", "z", "core"), ("zh", "y")
    return jax.shard_map(
        per_device,
        mesh=fine,
        in_specs=(P(rows, cols), P(rows, cols), P(None, rows, None), P(rows, cols)),
        out_specs=P(None, rows, None),
        check_vma=False,
    )
```

```python
import functools

import jax
import jax.numpy as jnp
from jax import lax
from jax.experimental import pallas as pl
from jax.experimental.pallas import tpu as pltpu
from jax.sharding import Mesh
from jax.sharding import PartitionSpec as P

BF = jnp.bfloat16
F32 = jnp.float32
HALF = 32
BLOCK = 2 * HALF
ROWS = 128
LEVELS = 7
TOP = LEVELS - 1
NZ = 8
NY = 4
SLICE = BLOCK // NY
NAMES = ("x1", "x0", "z", "core", "zh", "y")
PARAMS = pltpu.CompilerParams(vmem_limit_bytes=16 * 2**20)
WHOLE = pl.BlockSpec(memory_space=pltpu.VMEM)
SCALARS = pl.BlockSpec(memory_space=pltpu.SMEM)


class Place:
    def __init__(self, me):
        index = me[0]
        self.y, self.core, self.z, self.x0 = index & 3, index >> 3 & 1, index >> 4 & 7, index >> 7 & 1
        self.first_row = (index >> 3) * ROWS


def dot(a, b):
    return lax.dot_general(a, b, (((1,), (0,)), ((), ())), preferred_element_type=F32)


def iota(shape, dim):
    return lax.broadcasted_iota(jnp.int32, shape, dim)


def flips(count, distance=1):
    return [(i, i ^ distance) for i in range(count)]


def units(level):
    if level == 2:
        return [[(2 * z, 2 * z + 1)] for z in range(NZ)]
    if level < 2 or level == TOP:
        return [[(2 * z, None), (2 * z + 1, None)] for z in range(NZ)]
    bit = level - 3
    lows = [z for z in range(NZ) if not z >> bit & 1]
    return [[(2 * z + c, 2 * (z | 1 << bit) + c) for c in range(2)] for z in lows]


def pack_kernel(me, upstream, factors, out, wide, mix, turned, in_sems, mix_sems, out_sems):
    place = Place(me)
    blocks = turned.shape[0]
    chunk = turned.shape[1] - BLOCK
    tiles = wide.shape[1] // ROWS
    count = in_sems.shape[0]
    edges = [ROWS * (tiles * i // count) for i in range(count + 1)]
    loads = [
        pltpu.make_async_copy(upstream.at[:, lo:hi], wide.at[:, lo:hi], in_sems.at[i])
        for i, (lo, hi) in enumerate(zip(edges, edges[1:]))
    ]
    levels = [jnp.minimum(2 * place.y + side, TOP) for side in range(2)]
    load_mix = [pltpu.make_async_copy(factors.at[level], mix.at[i], mix_sems.at[i]) for i, level in enumerate(levels)]
    for load in load_mix + loads:
        load.start()
    for load in load_mix:
        load.wait()
    row = place.first_row + iota((BLOCK, ROWS), 1)
    sides = []
    for side, level in enumerate(levels):
        pick = lax.shift_right_logical(row, level + 5) % 2 * HALF + row % HALF
        sides.append((iota((BLOCK, ROWS), 0) == pick).astype(F32) + mix[side])
    sides[1] = jnp.where(place.y == NY - 1, pltpu.roll(sides[1], BLOCK, 1), sides[1])
    tile = jnp.concatenate(sides, axis=0).T.astype(BF)
    for block in range(blocks):
        half = block % 2 * BLOCK
        turned[block, chunk:] = tile[half : half + BLOCK]
    stores = []
    group = blocks // out_sems.shape[0]
    for t in range(tiles):
        if t * ROWS in edges:
            loads[edges.index(t * ROWS)].wait()
        columns = wide[:, t * ROWS : (t + 1) * ROWS].T
        start, end = t * ROWS, (t + 1) * ROWS
        while start < end:
            block, at = start // chunk, start % chunk
            size = min(end - start, chunk - at)
            turned[block, at : at + size] = columns[start - t * ROWS : start - t * ROWS + size]
            start += size
        while len(stores) < out_sems.shape[0] and end >= (len(stores) + 1) * group * chunk:
            at = slice(len(stores) * group, (len(stores) + 1) * group)
            stores.append(pltpu.make_async_copy(turned.at[at], out.at[at], out_sems.at[len(stores)]))
            stores[-1].start()
    for store in stores:
        store.wait()


def pack(me, upstream, factors):
    rows, wide = upstream.shape
    shape = (2 * NZ, wide // (2 * NZ) + BLOCK, rows)
    hbm = pl.BlockSpec(memory_space=pltpu.HBM)
    return pl.pallas_call(
        pack_kernel,
        in_specs=[SCALARS, hbm, hbm],
        out_specs=hbm,
        out_shape=jax.ShapeDtypeStruct(shape, BF),
        scratch_shapes=[
            pltpu.VMEM((rows, wide), BF),
            pltpu.VMEM((2,) + factors.shape[1:], F32),
            pltpu.VMEM(shape, BF),
            pltpu.SemaphoreType.DMA((4,)),
            pltpu.SemaphoreType.DMA((2,)),
            pltpu.SemaphoreType.DMA((4,)),
        ],
        compiler_params=pltpu.CompilerParams(vmem_limit_bytes=58 * 2**20),
        name="pack",
    )(me, upstream, factors)


def stack_kernel(me, *refs):
    *parts, _, out, top = refs
    place = Place(me)
    for k, part in enumerate(parts):
        out[k] = part[...]
    which = jnp.bitwise_xor(place.y, NY - 1)
    src, col = iota((ROWS, ROWS), 0), iota((ROWS, ROWS), 1)
    for h in range(2):
        picks = []
        for j in range(4):
            pick = (col // HALF == j) & (src == h * BLOCK + HALF * (1 - place.x0) + col % HALF)
            picks.append(pick.astype(F32).astype(BF))
        count = top.shape[0] // 2
        for k in range(count):
            packed = dot(out[which, 4 * k], picks[0])
            for j in range(1, 4):
                packed = packed + dot(out[which, 4 * k + j], picks[j])
            top[h * count + k] = packed.astype(BF)


def stack(me, parts, after):
    blocks, rows, wide = parts[0].shape
    return pl.pallas_call(
        stack_kernel,
        in_specs=[SCALARS] + [WHOLE] * NY + [pl.BlockSpec(memory_space=pl.ANY)],
        out_specs=[WHOLE] * 2,
        out_shape=[
            jax.ShapeDtypeStruct((NY, blocks, rows, wide), BF),
            jax.ShapeDtypeStruct((blocks // 2, rows, wide), BF),
        ],
        compiler_params=PARAMS,
        name="stack",
    )(me, *parts, after)


def spreader(level, my_x):
    width = 2 * ROWS if 2 <= level < TOP else ROWS
    src, col = iota((ROWS, width), 0), iota((ROWS, width), 1)
    lane = level % 2 * BLOCK
    parts = 2 if level == 1 else 4
    keep = (src // HALF) % parts == (col // HALF) % parts
    if level == 0:
        picks, keep = [src == lane + col % BLOCK], src // BLOCK == col // BLOCK
    elif level == 1:
        picks = [src == lane + col // BLOCK * HALF + col % HALF]
    elif level < TOP:
        picks = [src == lane + col // ROWS * HALF + col % HALF]
    else:
        picks = [src == HALF * my_x + col % HALF] + [src == HALF * j + col % HALF for j in range(4)]
    return [pick.astype(F32).astype(BF) for pick in picks], keep


def top_kernel(me, near, halves, mine, theirs, out, held, full, sem):
    place = Place(me)
    first_core = place.core == 0
    load = pltpu.make_async_copy(near.at[jnp.bitwise_xor(place.y, NY - 1)], held, sem)
    load.start()
    load.wait()
    src, col = iota((ROWS, ROWS), 0), iota((ROWS, ROWS), 1)
    keep = src // HALF == col // HALF
    own = [(src == h * BLOCK + HALF * place.x0 + col % HALF).astype(F32).astype(BF) for h in range(2)]
    far = [(src == HALF * j + col % HALF).astype(F32).astype(BF) for j in range(4)]
    count = halves.shape[0] // 2

    def rows(one, other):
        low, high = jnp.where(first_core, one, other), jnp.where(first_core, other, one)
        return jnp.where(keep, jnp.concatenate([low, high], axis=0), 0.0).astype(BF)

    for block in range(2 * NZ):
        k, pick = block // 4, far[block % 4]
        full[block, :ROWS] = rows(dot(held[block], own[0]), dot(held[block], own[1]))
        full[block, ROWS:] = rows(dot(halves[k], pick), dot(halves[count + k], pick))
    for block in range(2 * NZ):
        both = jnp.concatenate([mine[block], theirs[block]], axis=1)
        out[block] = dot(both, full[block]).astype(BF)


def top_grad(me, near, halves, mine, theirs):
    return pl.pallas_call(
        top_kernel,
        in_specs=[SCALARS, pl.BlockSpec(memory_space=pl.ANY)] + [WHOLE] * 3,
        out_specs=WHOLE,
        out_shape=jax.ShapeDtypeStruct(mine.shape, BF),
        scratch_shapes=[
            pltpu.VMEM(near.shape[1:], BF),
            pltpu.VMEM((2 * NZ, 2 * ROWS, ROWS), BF),
            pltpu.SemaphoreType.DMA,
        ],
        compiler_params=PARAMS,
        cost_estimate=pl.CostEstimate(flops=10**10, bytes_accessed=10**7, transcendentals=0),
        name="top_grad",
    )(me, near, halves, mine, theirs)


def spread(level, place, whole, dense):
    picks, keep = spreader(level, place.x0)
    for block in range(2 * NZ):
        full = dot(whole(block), picks[0])
        dense[block, :, : full.shape[1]] = jnp.where(keep, full, 0.0).astype(BF)


def dense_shape(level):
    return jax.ShapeDtypeStruct((2 * NZ, ROWS, ROWS if level < 2 else 2 * ROWS), BF)


def expand_kernel(me, near, away, _, *refs):
    dense, held, sems = refs[:TOP], refs[TOP:-1], refs[-1]
    place = Place(me)
    first_core = place.core == 0
    loads = [
        [
            pltpu.make_async_copy(ref.at[jnp.bitwise_xor(place.y, j)], held[c].at[j], sems.at[j, c])
            for c, ref in enumerate((near, away))
        ]
        for j in range(TOP // 2)
    ]
    for pair in loads:
        for load in pair:
            load.start()

    for level in range(TOP):
        j = level // 2
        if level % 2 == 0:
            for load in loads[j]:
                load.wait()

        def whole(block):
            one, other = held[0][j, block], held[1][j, block]
            return jnp.concatenate([jnp.where(first_core, one, other), jnp.where(first_core, other, one)], axis=0)

        spread(level, place, whole, dense[level])


def expand(me, near, away, after):
    held = pltpu.VMEM((TOP // 2,) + near.shape[1:], BF)
    return pl.pallas_call(
        expand_kernel,
        in_specs=[SCALARS] + [pl.BlockSpec(memory_space=pl.ANY)] * 3,
        out_specs=[WHOLE] * TOP,
        out_shape=[dense_shape(level) for level in range(TOP)],
        scratch_shapes=[held, held, pltpu.SemaphoreType.DMA((TOP // 2, 2))],
        compiler_params=PARAMS,
        name="expand",
    )(me, near, away, after)


def grad_step(level, mix, above, below):
    for lo, hi in [pair for unit in units(level) for pair in unit]:
        if level == 1:
            both, full = above[lo], mix[lo]
        else:
            both = jnp.concatenate([above[lo], above[hi]], axis=1)
            full = jnp.concatenate([mix[lo], mix[hi]], axis=0)
        out = dot(both, full).astype(BF)
        below[lo] = out[:, :ROWS]
        if hi is not None:
            below[hi] = out[:, ROWS:]


def forward_step(level, mix, x_ref, after):
    for lo, hi in [pair for unit in units(level) for pair in unit]:
        if hi is None:
            after[lo] = dot(mix[lo], x_ref[lo]).astype(BF)
        else:
            x = jnp.concatenate([x_ref[lo], x_ref[hi]], axis=0)
            both = dot(jnp.concatenate([mix[lo], mix[hi]], axis=0), x).astype(BF)
            after[lo], after[hi] = both[:ROWS], both[ROWS:]


def fold(quad):
    lane = iota((HALF, ROWS), 1) // HALF
    out = quad[:HALF]
    for q in range(1, 4):
        out = jnp.where(lane == q, quad[q * HALF : (q + 1) * HALF], out)
    return out


def products(level, core, x_ref, grads, mine, theirs, out):
    def store(z, halves):
        for y in range(NY):
            piece = halves[y // 2][y % 2 * SLICE : (y % 2 + 1) * SLICE]
            out[y, z, level] = piece.astype(BF)

    if level < 3 or level == TOP:
        for z in range(NZ):
            block = 2 * z + core
            if level == TOP:
                quad = dot(x_ref[block], jnp.concatenate([mine[block], theirs[block]], axis=1))
                store(z, (fold(quad[:, :ROWS]), fold(quad[:, ROWS:])))
            elif level == 2:
                quad = dot(jnp.concatenate([x_ref[2 * z], x_ref[2 * z + 1]], axis=0), grads[level][block])
                store(z, (fold(quad[:ROWS]), fold(quad[ROWS:])))
            elif level == 1:
                quad = dot(x_ref[block], grads[level][block])
                even = (iota((HALF, ROWS), 1) // HALF) % 2 == 0
                rows = [quad[q * HALF : (q + 1) * HALF] for q in range(4)]
                store(z, (jnp.where(even, rows[0], rows[1]), jnp.where(even, rows[2], rows[3])))
            else:
                quad = dot(x_ref[block], grads[level][block])
                both = jnp.where(iota((BLOCK, ROWS), 1) < BLOCK, quad[:BLOCK], quad[BLOCK:])
                store(z, (both[:HALF], both[HALF:]))
        return
    bit = level - 3
    for lo in [z for z in range(NZ) if not z >> bit & 1]:
        hi = lo | 1 << bit
        x = jnp.concatenate([x_ref[2 * lo + core], x_ref[2 * hi + core]], axis=0)
        g = jnp.concatenate([grads[level][2 * lo + core], grads[level][2 * hi + core]], axis=1)
        quad = dot(x, g)
        for z, at in ((lo, slice(0, ROWS)), (hi, slice(ROWS, 2 * ROWS))):
            store(z, (fold(quad[:ROWS, at]), fold(quad[ROWS:, at])))


def chain_kernel(me, base, *refs):
    dense, (top, mine, theirs, out) = refs[:TOP], refs[TOP : TOP + 4]
    grads, states = refs[TOP + 4 : 2 * TOP + 3] + (top,), refs[2 * TOP + 3 :]
    other = 1 - Place(me).core
    for block in range(2 * NZ):
        states[0][block] = base[block].T
    for step in range(TOP):
        level = TOP - 1 - step
        if level:
            grad_step(level, dense[level], grads[level], grads[level - 1])
        forward_step(step, dense[step], states[step], states[step + 1])
    for level in range(LEVELS):
        products(level, other, states[level], grads, mine, theirs, out)


def own_kernel(me, *refs):
    states, grads = refs[:LEVELS], refs[LEVELS : LEVELS + TOP]
    mine, theirs, out = refs[LEVELS + TOP :]
    for level in range(LEVELS):
        products(level, Place(me).core, states[level], grads, mine, theirs, out)


def chains(me, base, dense, top, mine, theirs):
    blocks, wide, rows = base.shape
    results = pl.pallas_call(
        chain_kernel,
        in_specs=[SCALARS] + [WHOLE] * (TOP + 4),
        out_specs=[WHOLE] * (TOP + LEVELS),
        out_shape=[jax.ShapeDtypeStruct((NY, NZ, LEVELS, SLICE, rows), BF)]
        + [jax.ShapeDtypeStruct(base.shape, BF)] * (TOP - 1)
        + [jax.ShapeDtypeStruct((blocks, rows, wide), BF)] * LEVELS,
        compiler_params=PARAMS,
        name="chains",
    )(me, base, *dense, top, mine, theirs)
    return results[0], [*results[1:TOP], top], results[TOP:]


def own_products(me, states, grads, mine, theirs):
    rows = mine.shape[2]
    return pl.pallas_call(
        own_kernel,
        in_specs=[SCALARS] + [WHOLE] * (LEVELS + TOP + 2),
        out_specs=WHOLE,
        out_shape=jax.ShapeDtypeStruct((NY, NZ, LEVELS, SLICE, rows), BF),
        compiler_params=PARAMS,
        name="own_products",
    )(me, *states, *grads, mine, theirs)


def call(kernel, shape, *args):
    return pl.pallas_call(
        kernel,
        in_specs=[SCALARS] + [WHOLE] * (len(args) - 1),
        out_specs=WHOLE,
        out_shape=shape,
        compiler_params=PARAMS,
        name=kernel.__name__,
    )(*args)


def core_sum(me, own, got, out):
    for y in range(NY):
        out[y] = (own[y].astype(F32) + got[y].astype(F32)).astype(BF)


def copies_of_sum(me, parts, out):
    total = parts[0].astype(F32)
    for k in range(1, parts.shape[0]):
        total = total + parts[k].astype(F32)
    for k in range(out.shape[0]):
        out[k] = total.astype(out.dtype)


def finish(me, slices, out):
    my_x = Place(me).x0
    own, other = my_x * NY, (1 - my_x) * NY
    for y in range(NY):
        at = slice(y * SLICE, (y + 1) * SLICE)
        out[:TOP, at] = slices[own + y, :TOP].astype(F32)
    near = [slices[own + y, TOP].astype(F32) for y in range(NY // 2)]
    far = [slices[other + y, TOP].astype(F32) for y in range(NY // 2, NY)]
    for h, (even, odd) in enumerate(((near, far), (far, near))):
        for y in range(NY // 2):
            at = h * HALF + y * SLICE
            out[TOP, at : at + SLICE] = jnp.where(my_x == 0, even[y], odd[y])


def per_device(codes, scales, factors, upstream):
    rows, wide = codes.shape
    blocks = 2 * NZ
    chunk = wide // blocks
    me = lax.axis_index(NAMES).astype(jnp.int32).reshape(1)

    got = lax.all_to_all(pack(me, upstream, factors.transpose(0, 2, 1)), ("z", "core"), 0, 0)
    mine, mixing = got[:, :chunk], got[:, chunk:]
    base = codes.astype(F32).reshape(rows, wide // rows, rows) * scales[0][None, :, None]
    base = base.reshape(rows, wide).astype(BF).T.reshape(blocks, chunk, rows)
    base = lax.all_to_all(base, ("z", "core"), 0, 0)
    theirs = lax.ppermute(mine, "x0", flips(2))

    near = [mixing] + [lax.ppermute(mixing, "y", flips(NY, k)) for k in range(1, NY)]
    near, top = stack(me, near, theirs)
    away = lax.ppermute(near, "core", flips(2))
    halves = lax.ppermute(top, "x0", flips(2))
    top = top_grad(me, near, halves, mine, theirs)
    dense = expand(me, near, away, base)
    away, grads, states = chains(me, base, dense, top, mine, theirs)
    got = lax.ppermute(away, "core", flips(2))
    own = own_products(me, states, grads, mine, theirs)

    part = (LEVELS, SLICE, rows)
    total = call(core_sum, jax.ShapeDtypeStruct(own.shape, BF), me, own, got)
    total = lax.all_to_all(total, "y", 0, 0)
    total = call(copies_of_sum, jax.ShapeDtypeStruct((2, NZ) + part, BF), me, total)
    total = lax.all_to_all(total.reshape((2 * NZ,) + part), ("zh", "z"), 0, 0)
    total = call(copies_of_sum, jax.ShapeDtypeStruct((2 * NY,) + part, BF), me, total)
    total = lax.all_to_all(total, ("x0", "y"), 0, 0)
    total = call(finish, jax.ShapeDtypeStruct((LEVELS, BLOCK, rows), F32), me, total)
    return total.transpose(0, 2, 1)


def solution(mesh):
    fsdp, col = mesh.devices.shape
    fine = Mesh(mesh.devices.reshape(fsdp // (4 * NZ), 2, NZ, 2, col // NY, NY), NAMES)
    rows, cols = ("x1", "x0", "z", "core"), ("zh", "y")
    return jax.shard_map(
        per_device,
        mesh=fine,
        in_specs=(P(rows, cols), P(rows, cols), P(None, rows, None), P(rows, cols)),
        out_specs=P(None, rows, None),
        check_vma=False,
    )
```
